512 devices in a mesh: section: 2 (over x_lo), dp: 32 (over x_hi, z, core), tensor: 8 (over y).
Axes of the slice: x: 4 (x_hi: 2, x_lo: 2; x = x_hi * 2 + x_lo), y: 8, z: 8, core: 2. Of those that a mesh axis runs over, the one named last changes fastest.
Arguments:
- inputs: bfloat16 [2, 256, 8192], P(None, 'section', 'tensor'), may hold values from -6 to 6
- gain: float32 [8192], P('tensor'), may hold values from 0.1 to 1.9
- w_first: bfloat16 [8192, 16384], P('tensor', 'dp'), may hold values from -0.0625 to 0.0625
- w_second: bfloat16 [16384, 8192], P('dp', 'tensor'), may hold values from -0.046875 to 0.046875
- cotangent: bfloat16 [2, 256, 8192], P(None, ('section', 'dp'), 'tensor'), may hold values from -6 to 6
Outputs:
- outputs: bfloat16 [2, 256, 8192], P(None, ('section', 'dp'), 'tensor')
- input_grad: bfloat16 [2, 256, 8192], P(None, ('section', 'dp'), 'tensor')
- first_grad: bfloat16 [8192, 16384], P('tensor', 'dp')
- second_grad: bfloat16 [16384, 8192], P('dp', 'tensor')
- gain_grad: float32 [8192], P('tensor')
The draws below stay inside these ranges and needn't reach their ends.
All inputs are finite; a program needn't handle non-finite values.
Results may differ from the reference program's by a relative error of at most 0.0067.
Values may be sent and summed in bfloat16 or wider, within the bound.
A program may use at most 64 MiB of HBM per device.

```python
import jax
import jax.numpy as jnp
from jax import lax

D = 8192
F = 16384
TOK_GRP = 128
MICRO = 2
TOKENS = 256
N_SECTION = 2


def level_of(key, shape, pieces, least, largest):
    factor_of = 1.0
    for dim, shards_of in pieces:
        steps = jax.random.uniform(jax.random.fold_in(jax.random.fold_in(key, 6), dim), (shards_of,), jnp.float32, least / len(pieces), largest / len(pieces))
        factor_of = factor_of * jnp.repeat(jnp.exp(steps), shape[dim] // shards_of).reshape((-1,) + (1,) * (len(shape) - 1 - dim))
    return factor_of


def normal_values(rng, dims, width, reach, split=(), held_as=jnp.bfloat16):
    level = level_of(rng, dims, split, -0.22, 0.18) if split else 1.0
    values = jax.random.normal(rng, dims, jnp.float32) * width * level
    return jnp.minimum(jnp.maximum(values, -reach), reach).astype(held_as)


def setup_inputs(seed: int = 0) -> dict:
    streams_of = jax.random.split(jax.random.key(seed), 6)
    return {
        "inputs": normal_values(streams_of[0], (MICRO, TOKENS, D), 1.0, 6.0, ((1, 2), (2, 8))),
        "gain": jnp.clip(1.0 + 0.18 * jax.random.normal(streams_of[1], (D,), jnp.float32), 0.1, 1.9),
        "w_first": normal_values(streams_of[2], (D, F), D ** -0.5, 0.0625, ((0, 8), (1, 32))),
        "w_second": normal_values(streams_of[3], (F, D), F ** -0.5, 0.046875, ((0, 32), (1, 8))),
        "cotangent": normal_values(streams_of[4], (MICRO, TOKENS, D), 1.0, 6.0, ((1, 64), (2, 8))),
    }


EPSILON = 1e-06

def reference(inputs, gain, w_first, w_second, cotangent):
    values = inputs.astype(jnp.float32)
    scale = lax.rsqrt(lax.optimization_barrier(jnp.mean(values * values, -1, keepdims=True)) + EPSILON)
    normed = (values * scale * gain).astype(jnp.bfloat16)
    flat_normed = normed.reshape(-1, D)
    pre = jnp.dot(flat_normed, w_first, preferred_element_type=jnp.float32)
    sig = jax.nn.sigmoid(pre)
    hidden = (pre * sig).astype(jnp.bfloat16)
    branch = jnp.dot(hidden, w_second, preferred_element_type=jnp.float32).reshape(values.shape)
    outputs = (values + branch).astype(jnp.bfloat16)
    flat_cot = cotangent.reshape(-1, D)
    hidden_grad = jnp.dot(flat_cot, w_second.T, preferred_element_type=jnp.float32)
    pre_grad = (hidden_grad * sig * (1.0 + pre * (1.0 - sig))).astype(jnp.bfloat16)
    normed_grad = jnp.dot(pre_grad, w_first.T, preferred_element_type=jnp.float32).reshape(values.shape)
    inner = lax.optimization_barrier(jnp.sum(values * gain * normed_grad, -1, keepdims=True))
    input_grad = (cotangent.astype(jnp.float32) + scale * gain * normed_grad - values * scale ** 3 * inner / D).astype(jnp.bfloat16)
    gain_grad = lax.optimization_barrier(jnp.sum(normed_grad * values * scale, axis=(0, 1)))

    def group_rows(array, group):
        shaped = array.reshape(MICRO, N_SECTION, TOK_GRP, array.shape[-1])
        return shaped[:, group].reshape(-1, array.shape[-1])
    first_grad = jnp.zeros((D, F), jnp.float32)
    second_grad = jnp.zeros((F, D), jnp.float32)
    for group in range(N_SECTION):
        part_second = jnp.dot(group_rows(hidden, group).T, group_rows(flat_cot, group), preferred_element_type=jnp.float32)
        part_first = jnp.dot(group_rows(flat_normed, group).T, group_rows(pre_grad, group), preferred_element_type=jnp.float32)
        second_grad = second_grad + lax.optimization_barrier(part_second.astype(jnp.bfloat16)).astype(jnp.float32)
        first_grad = first_grad + lax.optimization_barrier(part_first.astype(jnp.bfloat16)).astype(jnp.float32)
    return (outputs, input_grad, first_grad.astype(jnp.bfloat16), second_grad.astype(jnp.bfloat16), gain_grad)
```

```python
import jax
import jax.numpy as jnp
from jax import lax
from jax.experimental import pallas as pl
from jax.experimental.pallas import tpu as pltpu
from jax.sharding import PartitionSpec as P

MESH = pl.DeviceIdType.MESH
F32 = jnp.float32
BF16 = jnp.bfloat16
D = 8192
EPSILON = 1e-06
N = 8
HID = 512
FEAT = 1024
EXT = HID + 128
WIDE = FEAT + 128
NT = (((1,), (1,)), ((), ()))
TN = (((0,), (0,)), ((), ()))


class Phase:
    count = 0

    def __init__(self, make, first, last, sems):
        self.make, self.first, self.last, self.sems = make, first, last, sems
        self.base = sems["used"]
        sems["used"] += last - first

    def copy(self, k):
        src, dst, device = self.make(k)
        place = self.base + k - self.first
        return pltpu.make_async_remote_copy(
            src_ref=src,
            dst_ref=dst,
            send_sem=self.sems["send"].at[place],
            recv_sem=self.sems["recv"].at[place],
            device_id=device,
            device_id_type=MESH,
        )

    def _each(self, what):
        if self.last - self.first == 1:
            what(self.copy(self.first))
            return

        def body(k, carry):
            what(self.copy(k))
            return carry

        lax.fori_loop(self.first, self.last, body, 0)

    def start(self):
        self.sems["phases"].append(self)
        self._each(lambda c: c.start())

    def arrived(self):
        self._each(lambda c: c.wait_recv())

    def sent(self):
        self._each(lambda c: c.wait_send())


COPIES = 160


def kernel(
    x_hbm, gain_ref, w1_hbm, w2_hbm, cot_ref,
    out_ref, ing_ref, first_hbm, second_hbm, gg_ref,
    x_in, w1, w2, xp, u, u_o, cg, cg_o,
    s_a, r_a, s_sq, r_sq, s_c, r_c, hid, hid_o, q, q_o, p_own, slope, scl,
    branch, r_fs, s_fz, r_fz, s_fx, r_fx,
    big, r_gs, s_gz, r_gz, s_gx, r_gx,
    gsum, g_sib, g_s2, g_lo, g_s4, g_z, g_s8, g_xh,
    first_out, second_out,
    send_sems, recv_sems, local_sems,
):
    s = lax.axis_index("section")
    d = lax.axis_index("dp")
    t = lax.axis_index("tensor")
    xh = d // 16
    z = lax.rem(d // 2, N)
    c = lax.rem(d, 2)

    def y_peer(k):
        return {"section": s, "dp": d, "tensor": lax.rem(t + k, N)}

    def z_place(k):
        return lax.rem(z + k, N)

    def z_peer(k):
        return {"section": s, "dp": xh * 16 + z_place(k) * 2 + c, "tensor": t}

    xh_peer = {"section": s, "dp": lax.rem(d + 16, 32), "tensor": t}
    sib_peer = {"section": s, "dp": d + 1 - 2 * c, "tensor": t}
    lo_peer = {"section": 1 - s, "dp": d, "tensor": t}

    sems = {"used": 0, "send": send_sems, "recv": recv_sems, "phases": []}

    load_x = pltpu.make_async_copy(x_hbm, x_in, local_sems.at[0])
    load_w1 = pltpu.make_async_copy(w1_hbm, w1, local_sems.at[1])
    load_w2 = pltpu.make_async_copy(w2_hbm, w2, local_sems.at[2])
    load_x.start()
    load_w1.start()
    load_w2.start()

    barrier = pltpu.get_barrier_semaphore()

    def greet(k, carry):
        pl.semaphore_signal(barrier, inc=1, device_id=y_peer(k), device_id_type=MESH)
        pl.semaphore_signal(barrier, inc=1, device_id=z_peer(k), device_id_type=MESH)
        return carry

    lax.fori_loop(1, N, greet, 0)
    for peer in (xh_peer, sib_peer, lo_peer):
        pl.semaphore_signal(barrier, inc=1, device_id=peer, device_id_type=MESH)

    def y_rows(k):
        return pl.ds(pl.multiple_of(16 * lax.rem(t + k, N), 16), 16)

    my_rows = y_rows(0)
    mine = 16 + c * 8 + z
    other = c * 8 + z

    cot_own = jnp.concatenate([cot_ref[0].astype(F32), cot_ref[1].astype(F32)], axis=0)
    cg[mine] = cot_own.astype(BF16)

    row = lax.broadcasted_iota(jnp.int32, (256, 256), 0)
    col = lax.broadcasted_iota(jnp.int32, (256, 256), 1)
    half = row // 128
    x_half = jnp.where(half == 1, xh, 1 - xh)
    owner = x_half * 16 + (lax.rem(row, 64) // 8) * 2 + lax.rem(row, 128) // 64
    token = (lax.rem(row, 8) // 4) * 128 + owner * 4 + lax.rem(row, 4)
    perm = jnp.where(col == token, 1.0, 0.0).astype(BF16)
    load_x.wait()
    x_flat = x_in[...].reshape(256, FEAT)
    xs = jnp.dot(perm, x_flat, preferred_element_type=F32)
    xp[...] = xs
    gain = gain_ref[...]
    u[...] = (xs * gain).astype(BF16).reshape(2, 128, FEAT)

    ones = jnp.ones((8, FEAT), BF16)
    squares = []
    for h in range(2):
        rows = xp[h * 128 : (h + 1) * 128, :]
        sq = rows * rows
        hi = sq.astype(BF16)
        lo = (sq - hi.astype(F32)).astype(BF16)
        squares.append(
            lax.dot_general(ones, hi, NT, preferred_element_type=F32)
            + lax.dot_general(ones, lo, NT, preferred_element_type=F32)
        )
    place = lax.broadcasted_iota(jnp.int32, (8, 128), 0)
    s_sq[...] = jnp.where(place == 0, squares[0], squares[1])

    pl.semaphore_wait(barrier, 2 * (N - 1) + 3)

    to_xh = Phase(lambda k: (cg.at[mine], cg.at[other], xh_peer), 0, 1, sems)
    to_xh.start()
    to_z = Phase(lambda k: (cg.at[mine], cg.at[mine], z_peer(k)), 1, N, sems)
    to_z.start()
    sq_y = Phase(lambda k: (s_sq, r_sq.at[k], y_peer(k)), 1, N, sems)
    sq_y.start()

    load_w1.wait()
    s_a[...] = (
        jnp.dot(u[...].reshape(256, FEAT), w1[...], preferred_element_type=F32)
        .astype(BF16)
        .reshape(2, 128, HID)
    )
    a_y = Phase(lambda k: (s_a.at[:, y_rows(k)], r_a.at[k], y_peer(k)), 1, N, sems)
    a_y.start()

    to_xh.arrived()
    to_z2 = Phase(lambda k: (cg.at[other], cg.at[other], z_peer(k)), 1, N, sems)
    to_z2.start()
    core_rows = pl.ds(pl.multiple_of(64 * c, 64), 64)
    u_lo = Phase(lambda k: (u.at[:, core_rows], u_o.at[:, core_rows], lo_peer), 0, 1, sems)
    u_lo.start()

    def pieces(h):
        return pl.ds(h * 16 + c * 8, 8)

    def gathered(h):
        return Phase(lambda k: (cg.at[pieces(h)], cg.at[pieces(h)], sib_peer), 0, 1, sems)

    def crossed(h):
        return Phase(lambda k: (cg.at[pieces(h)], cg_o.at[pieces(h)], lo_peer), 0, 1, sems)

    load_w2.wait()
    to_z.arrived()
    cot_sib1 = gathered(1)
    cot_sib1.start()
    to_z2.arrived()
    cot_sib0 = gathered(0)
    cot_sib0.start()

    def rows_of(pieces_ref, h):
        return pieces_ref[h * 16 : (h + 1) * 16].astype(F32).reshape(128, FEAT).astype(BF16)

    c_y = [
        Phase(lambda k, h=h: (s_c.at[h, y_rows(k)], r_c.at[k, h], y_peer(k)), 1, N, sems)
        for h in range(2)
    ]
    for h, arrived in ((1, cot_sib1), (0, cot_sib0)):
        arrived.arrived()
        s_c[h] = lax.dot_general(
            rows_of(cg, h), w2[...], NT, preferred_element_type=F32
        ).astype(BF16)
        c_y[h].start()
    cot_lo = [crossed(0), crossed(1)]
    cot_lo[0].start()
    cot_lo[1].start()

    sq_y.arrived()
    a_y.arrived()
    total_sq = s_sq[...]
    for k in range(1, N):
        total_sq = total_sq + r_sq[k]
    lane = lax.broadcasted_iota(jnp.int32, (16, 128), 1)
    spot = lax.broadcasted_iota(jnp.int32, (16, 128), 0) + 16 * t
    for h in range(2):
        picked = jnp.where(lane == spot, jnp.broadcast_to(total_sq[h : h + 1, :], (16, 128)), 0.0)
        scale = lax.rsqrt(jnp.sum(picked, axis=1, keepdims=True) / D + EPSILON)
        sums = s_a[h, my_rows].astype(F32)
        for k in range(1, N):
            sums = sums + r_a[k, h].astype(F32)
        pre = sums * scale
        sig = jax.nn.sigmoid(pre)
        hid[h, my_rows] = (pre * sig).astype(BF16)
        p_own[h] = sums
        slope[h] = sig * (1.0 + pre * (1.0 - sig))
        scl[h] = jnp.broadcast_to(scale, (16, 128))
    b_y = Phase(lambda k: (hid.at[:, my_rows], hid.at[:, my_rows], y_peer(k)), 1, N, sems)
    b_y.start()

    d_y = [
        Phase(lambda k, h=h: (q.at[h, my_rows], q.at[h, my_rows], y_peer(k)), 1, N, sems)
        for h in range(2)
    ]
    for h in (1, 0):
        c_y[h].arrived()
        sums = s_c[h, my_rows].astype(F32)
        for k in range(1, N):
            sums = sums + r_c[k, h].astype(F32)
        scale = scl[h][:, :1]
        own = sums * slope[h] * scale
        q[h, my_rows, 0:HID] = own.astype(BF16)
        terms = own * p_own[h]
        lanes = terms[:, 0:128] + terms[:, 128:256] + terms[:, 256:384] + terms[:, 384:512]
        q[h, my_rows, HID:EXT] = (lanes * (scale * scale / D)).astype(BF16)
        d_y[h].start()

    b_y.arrived()
    hid_lo = Phase(lambda k: (hid, hid_o, lo_peer), 0, 1, sems)
    hid_lo.start()
    branch[...] = jnp.dot(
        hid[...].reshape(256, HID), w2[...], preferred_element_type=F32
    ).reshape(2, 128, FEAT)
    sib_rows = pl.ds(pl.multiple_of(64 - 64 * c, 64), 64)
    f_sib = Phase(lambda k: (branch.at[:, sib_rows], r_fs, sib_peer), 0, 1, sems)
    f_sib.start()

    u_lo.arrived()
    u_sib = Phase(lambda k: (u_o.at[:, core_rows], u_o.at[:, core_rows], sib_peer), 0, 1, sems)
    u_sib.start()

    f_sib.arrived()
    for h in range(2):
        both = branch[h, core_rows] + r_fs[h]
        s_fz[h] = both.reshape(N, 8, FEAT).astype(BF16)
    f_z = Phase(
        lambda k: (s_fz.at[:, z_place(k)], r_fz.at[k], z_peer(k)), 1, N, sems
    )
    f_z.start()

    g_sibs = [
        Phase(lambda k, h=h: (big.at[h, sib_rows], r_gs.at[h], sib_peer), 0, 1, sems)
        for h in range(2)
    ]
    g_zs = [
        Phase(lambda k, h=h: (s_gz.at[h, z_place(k)], r_gz.at[h, k], z_peer(k)), 1, N, sems)
        for h in range(2)
    ]
    q_lo = [
        Phase(lambda k, h=h: (q.at[h], q_o.at[h], lo_peer), 0, 1, sems)
        for h in range(2)
    ]
    gain_part = jnp.zeros((1, FEAT), F32)
    for h in range(2):
        d_y[h].arrived()
        part = lax.dot_general(q[h, :, 0:HID], w1[...], NT, preferred_element_type=F32)
        big[h, :, 0:FEAT] = part
        big[h, :, FEAT:WIDE] = q[h, :, HID:EXT].astype(F32)
        g_sibs[h].start()
        q_lo[h].start()
        gain_part = gain_part + jnp.sum(
            part * xp[h * 128 : (h + 1) * 128, :], axis=0, keepdims=True
        )
        g_sibs[h].arrived()
        both = big[h, core_rows] + r_gs[h]
        s_gz[h] = both.reshape(N, 8, WIDE).astype(BF16)
        g_zs[h].start()

    gsum[...] = gain_part
    gg_sib = Phase(lambda k: (gsum, g_sib, sib_peer), 0, 1, sems)
    gg_sib.start()

    cot_sibo = [
        Phase(lambda k, h=h: (cg_o.at[pieces(h)], cg_o.at[pieces(h)], sib_peer), 0, 1, sems)
        for h in range(2)
    ]
    for h in range(2):
        cot_lo[h].arrived()
        cot_sibo[h].start()
    gg_sib.arrived()
    g_s2[...] = gsum[...] + g_sib[...]
    gg_lo = Phase(lambda k: (g_s2, g_lo, lo_peer), 0, 1, sems)
    gg_lo.start()

    hid_lo.arrived()
    for h in range(2):
        cot_sibo[h].arrived()
    second = jnp.zeros((HID, FEAT), F32)
    hid_all = jnp.concatenate(
        [hid[...].reshape(256, HID), hid_o[...].reshape(256, HID)], axis=0
    )
    cot_all = jnp.concatenate(
        [rows_of(cg, 0), rows_of(cg, 1), rows_of(cg_o, 0), rows_of(cg_o, 1)], axis=0
    )
    second_out[...] = lax.dot_general(
        hid_all, cot_all, TN, preferred_element_type=F32
    ).astype(BF16)
    save_second = pltpu.make_async_copy(second_out, second_hbm, local_sems.at[3])
    save_second.start()

    gg_lo.arrived()
    g_s4[...] = g_s2[...] + g_lo[...]
    gg_z = Phase(lambda k: (g_s4, g_z.at[k], z_peer(k)), 1, N, sems)
    gg_z.start()

    f_z.arrived()

    def z_total(sent, received, h):
        total = sent[h, z].astype(F32)
        for k in range(1, N):
            total = total + received(k)
        return total

    s_fx[...] = z_total(s_fz, lambda k: r_fz[k, 0].astype(F32), 0)
    f_xh = Phase(lambda k: (s_fx, r_fx, xh_peer), 0, 1, sems)
    f_xh.start()
    own_branch = z_total(s_fz, lambda k: r_fz[k, 1].astype(F32), 1)

    g_zs[0].arrived()
    s_gx[...] = z_total(s_gz, lambda k: r_gz[0, k].astype(F32), 0)
    g_xhp = Phase(lambda k: (s_gx, r_gx, xh_peer), 0, 1, sems)
    g_xhp.start()

    u_sib.arrived()
    for h in range(2):
        q_lo[h].arrived()
    u_all = jnp.concatenate([u[...].reshape(256, FEAT), u_o[...].reshape(256, FEAT)], axis=0)
    q_all = jnp.concatenate(
        [q[0, :, 0:HID], q[1, :, 0:HID], q_o[0, :, 0:HID], q_o[1, :, 0:HID]], axis=0
    )
    first_out[...] = lax.dot_general(u_all, q_all, TN, preferred_element_type=F32).astype(BF16)
    save_first = pltpu.make_async_copy(first_out, first_hbm, local_sems.at[4])
    save_first.start()

    gg_z.arrived()
    gain_total = g_s4[...]
    for k in range(1, N):
        gain_total = gain_total + g_z[k]
    g_s8[...] = gain_total
    gg_xh = Phase(lambda k: (g_s8, g_xh, xh_peer), 0, 1, sems)
    gg_xh.start()

    x_own = xp[pl.ds(pl.multiple_of(mine * 8, 8), 8), :]
    f_xh.arrived()
    outputs = x_own + own_branch + r_fx[...]
    out_ref[0] = outputs[0:4].astype(BF16)
    out_ref[1] = outputs[4:8].astype(BF16)

    g_zs[1].arrived()
    normed_grad = z_total(s_gz, lambda k: r_gz[1, k].astype(F32), 1)
    g_xhp.arrived()
    normed_grad = normed_grad + r_gx[...]
    inner = jnp.sum(normed_grad[:, FEAT:WIDE], axis=1, keepdims=True)
    grads = cg[mine].astype(F32) + gain * normed_grad[:, 0:FEAT] - x_own * inner
    ing_ref[0] = grads[0:4].astype(BF16)
    ing_ref[1] = grads[4:8].astype(BF16)

    gg_xh.arrived()
    gg_ref[...] = g_s8[...] + g_xh[...]

    for phase in sems["phases"]:
        phase.sent()
    save_second.wait()
    save_first.wait()


def per_device(inputs, gain, w_first, w_second, cotangent):
    vmem = pl.BlockSpec(memory_space=pltpu.VMEM)
    hbm = pl.BlockSpec(memory_space=pl.ANY)
    shapes = [
        ((2, 128, FEAT), BF16),
        ((FEAT, HID), BF16),
        ((HID, FEAT), BF16),
        ((256, FEAT), F32),
        ((2, 128, FEAT), BF16),
        ((2, 128, FEAT), BF16),
        ((32, 8, FEAT), BF16),
        ((32, 8, FEAT), BF16),
        ((2, 128, HID), BF16),
        ((N, 2, 16, HID), BF16),
        ((8, 128), F32),
        ((N, 8, 128), F32),
        ((2, 128, HID), BF16),
        ((N, 2, 16, HID), BF16),
        ((2, 128, HID), BF16),
        ((2, 128, HID), BF16),
        ((2, 128, EXT), BF16),
        ((2, 128, EXT), BF16),
        ((2, 16, HID), F32),
        ((2, 16, HID), F32),
        ((2, 16, 128), F32),
        ((2, 128, FEAT), F32),
        ((2, 64, FEAT), F32),
        ((2, N, 8, FEAT), BF16),
        ((N, 2, 8, FEAT), BF16),
        ((8, FEAT), F32),
        ((8, FEAT), F32),
        ((2, 128, WIDE), F32),
        ((2, 64, WIDE), F32),
        ((2, N, 8, WIDE), BF16),
        ((2, N, 8, WIDE), BF16),
        ((8, WIDE), F32),
        ((8, WIDE), F32),
        ((1, FEAT), F32),
        ((1, FEAT), F32),
        ((1, FEAT), F32),
        ((1, FEAT), F32),
        ((1, FEAT), F32),
        ((N, 1, FEAT), F32),
        ((1, FEAT), F32),
        ((1, FEAT), F32),
        ((FEAT, HID), BF16),
        ((HID, FEAT), BF16),
    ]
    outputs, input_grad, first_grad, second_grad, gain_grad = pl.pallas_call(
        kernel,
        out_shape=(
            jax.ShapeDtypeStruct(cotangent.shape, BF16),
            jax.ShapeDtypeStruct(cotangent.shape, BF16),
            jax.ShapeDtypeStruct(w_first.shape, BF16),
            jax.ShapeDtypeStruct(w_second.shape, BF16),
            jax.ShapeDtypeStruct((1, FEAT), F32),
        ),
        in_specs=[hbm, vmem, hbm, hbm, vmem],
        out_specs=(vmem, vmem, hbm, hbm, vmem),
        scratch_shapes=[pltpu.VMEM(shape, dtype) for shape, dtype in shapes]
        + [
            pltpu.SemaphoreType.DMA((COPIES,)),
            pltpu.SemaphoreType.DMA((COPIES,)),
            pltpu.SemaphoreType.DMA((5,)),
        ],
        compiler_params=pltpu.CompilerParams(
            collective_id=0, has_side_effects=True, vmem_limit_bytes=48 * 1024 * 1024
        ),
    )(inputs, gain.reshape(1, FEAT), w_first, w_second, cotangent)
    return outputs, input_grad, first_grad, second_grad, gain_grad.reshape(FEAT)


def solution(mesh):
    in_specs = (
        P(None, "section", "tensor"),
        P("tensor"),
        P("tensor", "dp"),
        P("dp", "tensor"),
        P(None, ("section", "dp"), "tensor"),
    )
    out_specs = (
        P(None, ("section", "dp"), "tensor"),
        P(None, ("section", "dp"), "tensor"),
        P("tensor", "dp"),
        P("dp", "tensor"),
        P("tensor"),
    )
    return jax.shard_map(
        per_device, mesh=mesh, in_specs=in_specs, out_specs=out_specs, check_vma=False
    )
```

```python
import jax
import jax.numpy as jnp
from jax import lax
from jax.experimental import pallas as pl
from jax.experimental.pallas import tpu as pltpu
from jax.sharding import PartitionSpec as P

MESH = pl.DeviceIdType.MESH
F32 = jnp.float32
BF16 = jnp.bfloat16
D = 8192
EPSILON = 1e-06
N = 8
HID = 512
FEAT = 1024
ROW = FEAT + 256
NT = (((1,), (1,)), ((), ()))
TN = (((0,), (0,)), ((), ()))


class Phase:
    def __init__(self, make, first, last, sems):
        self.make, self.first, self.last, self.sems = make, first, last, sems
        self.base = sems["used"]
        sems["used"] += last - first

    def copy(self, k):
        src, dst, device = self.make(k)
        place = self.base + k - self.first
        return pltpu.make_async_remote_copy(
            src_ref=src,
            dst_ref=dst,
            send_sem=self.sems["send"].at[place],
            recv_sem=self.sems["recv"].at[place],
            device_id=device,
            device_id_type=MESH,
        )

    def _each(self, what):
        if self.last - self.first == 1:
            what(self.copy(self.first))
            return

        def body(k, carry):
            what(self.copy(k))
            return carry

        lax.fori_loop(self.first, self.last, body, 0)

    def start(self):
        self.sems["phases"].append(self)
        self._each(lambda c: c.start())

    def arrived(self):
        self._each(lambda c: c.wait_recv())

    def sent(self):
        self._each(lambda c: c.wait_send())


COPIES = 160


def kernel(
    x_hbm, gain_hbm, w1_hbm, w2_hbm, cot_hbm,
    out_ref, ing_ref, first_out, second_out, gg_ref,
    x_in, gain_ref, w1, w2, cot_ref, xp, u, u_o, cg, cg_o,
    s_a, r_a, s_sq, r_sq, s_c, r_c, hid, hid_o, q, q_o, p_own, slope, scl,
    branch, r_fs, s_fz, r_fz, s_fx, r_fx,
    big, r_gs, s_gz, r_gz, s_gx, r_gx,
    e_s, e_r, gg_own, gg_r1, gg_chip, gg_rz, gg_line, gg_rx,
    send_sems, recv_sems, local_sems,
):
    s = lax.axis_index("section")
    d = lax.axis_index("dp")
    t = lax.axis_index("tensor")
    xh = d // 16
    z = lax.rem(d // 2, N)
    c = lax.rem(d, 2)

    def y_peer(k):
        return {"section": s, "dp": d, "tensor": lax.rem(t + k, N)}

    def z_place(k):
        return lax.rem(z + k, N)

    def z_peer(k):
        return {"section": s, "dp": xh * 16 + z_place(k) * 2 + c, "tensor": t}

    xh_peer = {"section": s, "dp": lax.rem(d + 16, 32), "tensor": t}
    sib_peer = {"section": s, "dp": d + 1 - 2 * c, "tensor": t}
    lo_peer = {"section": 1 - s, "dp": d, "tensor": t}
    far_peer = {"section": 1 - s, "dp": lax.rem(d + 16, 32), "tensor": t}

    sems = {"used": 0, "send": send_sems, "recv": recv_sems, "phases": []}

    load_cot = pltpu.make_async_copy(cot_hbm, cot_ref, local_sems.at[0])
    load_gain = pltpu.make_async_copy(gain_hbm, gain_ref, local_sems.at[1])
    load_x = pltpu.make_async_copy(x_hbm, x_in, local_sems.at[2])
    load_w1 = pltpu.make_async_copy(w1_hbm, w1, local_sems.at[3])
    load_w2 = pltpu.make_async_copy(w2_hbm, w2, local_sems.at[4])
    for load in (load_cot, load_gain, load_x, load_w1, load_w2):
        load.start()

    barrier = pltpu.get_barrier_semaphore()

    def greet(k, carry):
        pl.semaphore_signal(barrier, inc=1, device_id=y_peer(k), device_id_type=MESH)
        pl.semaphore_signal(barrier, inc=1, device_id=z_peer(k), device_id_type=MESH)
        return carry

    lax.fori_loop(1, N, greet, 0)
    for peer in (xh_peer, sib_peer, lo_peer, far_peer):
        pl.semaphore_signal(barrier, inc=1, device_id=peer, device_id_type=MESH)

    def y_rows(k):
        return pl.ds(pl.multiple_of(16 * lax.rem(t + k, N), 16), 16)

    my_rows = y_rows(0)
    mine = 16 + c * 8 + z
    other = c * 8 + z

    load_cot.wait()
    cot_own = jnp.concatenate([cot_ref[0].astype(F32), cot_ref[1].astype(F32)], axis=0)
    cg[mine] = cot_own.astype(BF16)

    pl.semaphore_wait(barrier, 2 * (N - 1) + 4)

    to_xh = Phase(lambda k: (cg.at[mine], cg.at[other], xh_peer), 0, 1, sems)
    to_xh.start()
    to_z = Phase(lambda k: (cg.at[mine], cg.at[mine], z_peer(k)), 1, N, sems)
    to_z.start()

    row = lax.broadcasted_iota(jnp.int32, (256, 256), 0)
    col = lax.broadcasted_iota(jnp.int32, (256, 256), 1)
    x_half = jnp.where(row // 128 == 1, xh, 1 - xh)
    owner = x_half * 16 + (lax.rem(row, 64) // 8) * 2 + lax.rem(row, 128) // 64
    token = (lax.rem(row, 8) // 4) * 128 + owner * 4 + lax.rem(row, 4)
    perm = jnp.where(col == token, 1.0, 0.0).astype(BF16)
    load_x.wait()
    x_flat = x_in[...].reshape(256, FEAT)
    xs = jnp.dot(perm, x_flat, preferred_element_type=F32)
    xp[...] = xs
    load_gain.wait()
    gain = gain_ref[...]
    u[...] = (xs * gain).astype(BF16).reshape(2, 128, FEAT)
    load_w1.wait()
    s_a[...] = (
        jnp.dot(u[...].reshape(256, FEAT), w1[...], preferred_element_type=F32)
        .astype(BF16)
        .reshape(2, 128, HID)
    )
    a_y = Phase(lambda k: (s_a.at[:, y_rows(k)], r_a.at[k], y_peer(k)), 1, N, sems)
    a_y.start()

    ones = jnp.ones((8, FEAT), BF16)
    squares = []
    for h in range(2):
        rows = xp[h * 128 : (h + 1) * 128, :]
        sq = rows * rows
        hi = sq.astype(BF16)
        lo = (sq - hi.astype(F32)).astype(BF16)
        squares.append(
            lax.dot_general(ones, hi, NT, preferred_element_type=F32)
            + lax.dot_general(ones, lo, NT, preferred_element_type=F32)
        )
    place = lax.broadcasted_iota(jnp.int32, (8, 128), 0)
    s_sq[...] = jnp.where(place == 0, squares[0], squares[1])
    sq_y = Phase(lambda k: (s_sq, r_sq.at[k], y_peer(k)), 1, N, sems)
    sq_y.start()

    to_xh.arrived()
    to_z2 = Phase(lambda k: (cg.at[other], cg.at[other], z_peer(k)), 1, N, sems)
    to_z2.start()
    core_rows = pl.ds(pl.multiple_of(64 * c, 64), 64)
    u_lo = Phase(lambda k: (u.at[:, core_rows], u_o.at[:, core_rows], lo_peer), 0, 1, sems)
    u_lo.start()

    def pieces(h):
        return pl.ds(h * 16 + c * 8, 8)

    def gathered(h):
        return Phase(lambda k: (cg.at[pieces(h)], cg.at[pieces(h)], sib_peer), 0, 1, sems)

    def crossed(h):
        return Phase(lambda k: (cg.at[pieces(h)], cg_o.at[pieces(h)], lo_peer), 0, 1, sems)

    def rows_of(pieces_ref, h):
        return pieces_ref[h * 16 : (h + 1) * 16].astype(F32).reshape(128, FEAT).astype(BF16)

    c_y = [
        Phase(lambda k, h=h: (s_c.at[h, y_rows(k)], r_c.at[k, h], y_peer(k)), 1, N, sems)
        for h in range(2)
    ]

    def send_c(h):
        s_c[h] = lax.dot_general(
            rows_of(cg, h), w2[...], NT, preferred_element_type=F32
        ).astype(BF16)
        c_y[h].start()

    load_w2.wait()
    to_z.arrived()
    cot_sib1 = gathered(1)
    cot_sib1.start()
    cot_sib1.arrived()
    send_c(1)
    cot_lo1 = crossed(1)
    cot_lo1.start()

    sq_y.arrived()
    total_sq = s_sq[...]
    for k in range(1, N):
        total_sq = total_sq + r_sq[k]
    lane = lax.broadcasted_iota(jnp.int32, (16, 128), 1)
    spot = lax.broadcasted_iota(jnp.int32, (16, 128), 0) + 16 * t
    a_y.arrived()
    for h in range(2):
        picked = jnp.where(lane == spot, jnp.broadcast_to(total_sq[h : h + 1, :], (16, 128)), 0.0)
        scale = lax.rsqrt(jnp.sum(picked, axis=1, keepdims=True) / D + EPSILON)
        sums = s_a[h, my_rows].astype(F32)
        for k in range(1, N):
            sums = sums + r_a[k, h].astype(F32)
        pre = sums * scale
        sig = jax.nn.sigmoid(pre)
        hid[h, my_rows] = (pre * sig).astype(BF16)
        p_own[h] = sums
        slope[h] = sig * (1.0 + pre * (1.0 - sig))
        scl[h] = jnp.broadcast_to(scale, (16, 128))

    b_near = Phase(
        lambda k: (hid.at[:, my_rows], hid.at[:, my_rows], y_peer(1 + 6 * k)), 0, 2, sems
    )
    b_near.start()

    to_z2.arrived()
    cot_sib0 = gathered(0)
    cot_sib0.start()
    cot_sib0.arrived()
    send_c(0)
    cot_lo0 = crossed(0)
    cot_lo0.start()

    b_near.arrived()
    left_rows, right_rows = y_rows(N - 1), y_rows(1)
    b_right = Phase(
        lambda k: (hid.at[:, left_rows], hid.at[:, left_rows], y_peer(k)), 1, 3, sems
    )
    b_left = Phase(
        lambda k: (hid.at[:, right_rows], hid.at[:, right_rows], y_peer(N - k)), 1, 3, sems
    )
    b_right3 = Phase(
        lambda k: (hid.at[0, left_rows], hid.at[0, left_rows], y_peer(3)), 0, 1, sems
    )
    b_left3 = Phase(
        lambda k: (hid.at[1, right_rows], hid.at[1, right_rows], y_peer(N - 3)), 0, 1, sems
    )
    b_rest = (b_right3, b_left3, b_right, b_left)
    for phase in b_rest:
        phase.start()

    d_y = [
        Phase(lambda k, h=h: (q.at[h, my_rows], q.at[h, my_rows], y_peer(k)), 1, N, sems)
        for h in range(2)
    ]
    for h in (1, 0):
        c_y[h].arrived()
        sums = s_c[h, my_rows].astype(F32)
        for k in range(1, N):
            sums = sums + r_c[k, h].astype(F32)
        scale = scl[h][:, :1]
        own = sums * slope[h] * scale
        q[h, my_rows] = own.astype(BF16)
        if h == 0:
            d_y[0].start()
            d_y[1].start()
        inner = jnp.sum(own * p_own[h], axis=1, keepdims=True) * (scale * scale / D)
        e_s[:, h * 128 : (h + 1) * 128] = jnp.sum(
            jnp.where(lane == spot, inner, 0.0), axis=0, keepdims=True
        )
    e_y = Phase(lambda k: (e_s, e_r.at[k], y_peer(k)), 1, N, sems)
    e_y.start()

    for phase in b_rest:
        phase.arrived()
    hid_lo = Phase(lambda k: (hid, hid_o, lo_peer), 0, 1, sems)
    hid_lo.start()
    branch[...] = jnp.dot(
        hid[...].reshape(256, HID), w2[...], preferred_element_type=F32
    ).reshape(2, 128, FEAT)
    sib_rows = pl.ds(pl.multiple_of(64 - 64 * c, 64), 64)
    f_sib = Phase(lambda k: (branch.at[:, sib_rows], r_fs, sib_peer), 0, 1, sems)
    f_sib.start()

    u_lo.arrived()
    u_sib = Phase(lambda k: (u_o.at[:, core_rows], u_o.at[:, core_rows], sib_peer), 0, 1, sems)
    u_sib.start()

    f_sib.arrived()
    for h in range(2):
        both = branch[h, core_rows] + r_fs[h]
        s_fz[h] = both.reshape(N, 8, FEAT).astype(BF16)
    f_z = Phase(
        lambda k: (s_fz.at[:, z_place(k)], r_fz.at[k], z_peer(k)), 1, N, sems
    )
    f_z.start()

    g_sibs = [
        Phase(lambda k, h=h: (big.at[h, sib_rows], r_gs.at[h], sib_peer), 0, 1, sems)
        for h in range(2)
    ]
    g_zs = [
        Phase(lambda k, h=h: (s_gz.at[h, z_place(k)], r_gz.at[h, k], z_peer(k)), 1, N, sems)
        for h in range(2)
    ]
    q_lo = [
        Phase(lambda k, h=h: (q.at[h], q_o.at[h], lo_peer), 0, 1, sems)
        for h in range(2)
    ]
    gain_part = jnp.zeros((1, FEAT), F32)
    for h in range(2):
        d_y[h].arrived()
        part = lax.dot_general(q[h], w1[...], NT, preferred_element_type=F32)
        big[h] = part
        g_sibs[h].start()
        q_lo[h].start()
        gain_part = gain_part + jnp.sum(
            part * xp[h * 128 : (h + 1) * 128, :], axis=0, keepdims=True
        )
        if h == 1:
            e_y.arrived()
            e_sum = e_s[...]
            for k in range(1, N):
                e_sum = e_sum + e_r[k]
            gg_own[:, 0:FEAT] = gain_part
            gg_own[:, FEAT:ROW] = e_sum
            gg_sib = Phase(lambda k: (gg_own, gg_r1, sib_peer), 0, 1, sems)
            gg_sib.start()
        g_sibs[h].arrived()
        both = big[h, core_rows] + r_gs[h]
        s_gz[h] = both.reshape(N, 8, FEAT).astype(BF16)
        g_zs[h].start()
    gg_sib.arrived()
    gg_chip[...] = gg_own[...] + gg_r1[...]
    gg_z = Phase(lambda k: (gg_chip, gg_rz.at[k], z_peer(k)), 1, N, sems)
    gg_z.start()

    cot_sibo = [
        Phase(lambda k, h=h: (cg_o.at[pieces(h)], cg_o.at[pieces(h)], sib_peer), 0, 1, sems)
        for h in range(2)
    ]
    cot_lo1.arrived()
    cot_sibo[1].start()
    cot_lo0.arrived()
    cot_sibo[0].start()
    hid_lo.arrived()
    for h in range(2):
        cot_sibo[h].arrived()
    hid_all = jnp.concatenate(
        [hid[...].reshape(256, HID), hid_o[...].reshape(256, HID)], axis=0
    )
    cot_all = jnp.concatenate(
        [rows_of(cg, 0), rows_of(cg, 1), rows_of(cg_o, 0), rows_of(cg_o, 1)], axis=0
    )
    second_out[...] = lax.dot_general(
        hid_all, cot_all, TN, preferred_element_type=F32
    ).astype(BF16)

    def z_total(sent, received, h):
        total = sent[h, z].astype(F32)
        for k in range(1, N):
            total = total + received(k)
        return total

    f_z.arrived()
    s_fx[...] = z_total(s_fz, lambda k: r_fz[k, 0].astype(F32), 0)
    f_xh = Phase(lambda k: (s_fx, r_fx, xh_peer), 0, 1, sems)
    f_xh.start()
    own_branch = z_total(s_fz, lambda k: r_fz[k, 1].astype(F32), 1)

    g_zs[0].arrived()
    s_gx[...] = z_total(s_gz, lambda k: r_gz[0, k].astype(F32), 0)
    g_xh = Phase(lambda k: (s_gx, r_gx, xh_peer), 0, 1, sems)
    g_xh.start()

    gg_z.arrived()
    gg_total = gg_chip[...]
    for k in range(1, N):
        gg_total = gg_total + gg_rz[k]
    gg_line[...] = gg_total
    gg_x = [
        Phase(lambda k, i=i, peer=peer: (gg_line, gg_rx.at[i], peer), 0, 1, sems)
        for i, peer in enumerate((xh_peer, lo_peer, far_peer))
    ]
    for phase in gg_x:
        phase.start()

    u_sib.arrived()
    for h in range(2):
        q_lo[h].arrived()
    u_all = jnp.concatenate([u[...].reshape(256, FEAT), u_o[...].reshape(256, FEAT)], axis=0)
    q_all = jnp.concatenate(
        [q[...].reshape(256, HID), q_o[...].reshape(256, HID)], axis=0
    )
    first_out[...] = lax.dot_general(u_all, q_all, TN, preferred_element_type=F32).astype(BF16)

    x_own = xp[pl.ds(pl.multiple_of(mine * 8, 8), 8), :]
    f_xh.arrived()
    outputs = x_own + own_branch + r_fx[...]
    out_ref[0] = outputs[0:4].astype(BF16)
    out_ref[1] = outputs[4:8].astype(BF16)

    g_zs[1].arrived()
    normed_grad = z_total(s_gz, lambda k: r_gz[1, k].astype(F32), 1)
    g_xh.arrived()
    normed_grad = normed_grad + r_gx[...]
    for phase in gg_x:
        phase.arrived()
    inner_row = gg_line[:, FEAT + 128 : ROW] + gg_rx[0][:, FEAT : FEAT + 128]
    own_lane = lax.broadcasted_iota(jnp.int32, (8, 128), 1)
    own_spot = lax.broadcasted_iota(jnp.int32, (8, 128), 0) + c * 64 + z * 8
    inner = jnp.sum(
        jnp.where(own_lane == own_spot, jnp.broadcast_to(inner_row, (8, 128)), 0.0),
        axis=1,
        keepdims=True,
    )
    grads = cg[mine].astype(F32) + gain * normed_grad - x_own * inner
    ing_ref[0] = grads[0:4].astype(BF16)
    ing_ref[1] = grads[4:8].astype(BF16)
    gg_ref[...] = (gg_line[:, 0:FEAT] + gg_rx[0][:, 0:FEAT]) + (
        gg_rx[1][:, 0:FEAT] + gg_rx[2][:, 0:FEAT]
    )

    for phase in sems["phases"]:
        phase.sent()


def save(*refs):
    sources, targets, sems = refs[:5], refs[5:10], refs[10]
    copies = [pltpu.make_async_copy(sources[i], targets[i], sems.at[i]) for i in range(5)]
    for copy in copies:
        copy.start()
    for copy in copies:
        copy.wait()


def per_device(inputs, gain, w_first, w_second, cotangent):
    vmem = pl.BlockSpec(memory_space=pltpu.VMEM)
    hbm = pl.BlockSpec(memory_space=pltpu.HBM)
    anywhere = pl.BlockSpec(memory_space=pl.ANY)
    shapes = [
        ((2, 128, FEAT), BF16),
        ((1, FEAT), F32),
        ((FEAT, HID), BF16),
        ((HID, FEAT), BF16),
        ((2, 4, FEAT), BF16),
        ((256, FEAT), F32),
        ((2, 128, FEAT), BF16),
        ((2, 128, FEAT), BF16),
        ((32, 8, FEAT), BF16),
        ((32, 8, FEAT), BF16),
        ((2, 128, HID), BF16),
        ((N, 2, 16, HID), BF16),
        ((8, 128), F32),
        ((N, 8, 128), F32),
        ((2, 128, HID), BF16),
        ((N, 2, 16, HID), BF16),
        ((2, 128, HID), BF16),
        ((2, 128, HID), BF16),
        ((2, 128, HID), BF16),
        ((2, 128, HID), BF16),
        ((2, 16, HID), F32),
        ((2, 16, HID), F32),
        ((2, 16, 128), F32),
        ((2, 128, FEAT), F32),
        ((2, 64, FEAT), F32),
        ((2, N, 8, FEAT), BF16),
        ((N, 2, 8, FEAT), BF16),
        ((8, FEAT), F32),
        ((8, FEAT), F32),
        ((2, 128, FEAT), F32),
        ((2, 64, FEAT), F32),
        ((2, N, 8, FEAT), BF16),
        ((2, N, 8, FEAT), BF16),
        ((8, FEAT), F32),
        ((8, FEAT), F32),
        ((1, 256), F32),
        ((N, 1, 256), F32),
        ((1, ROW), F32),
        ((1, ROW), F32),
        ((1, ROW), F32),
        ((N, 1, ROW), F32),
        ((1, ROW), F32),
        ((3, 1, ROW), F32),
    ]
    results = (
        jax.ShapeDtypeStruct(cotangent.shape, BF16),
        jax.ShapeDtypeStruct(cotangent.shape, BF16),
        jax.ShapeDtypeStruct(w_first.shape, BF16),
        jax.ShapeDtypeStruct(w_second.shape, BF16),
        jax.ShapeDtypeStruct((1, FEAT), F32),
    )
    made = pl.pallas_call(
        kernel,
        out_shape=results,
        in_specs=[hbm] * 5,
        out_specs=(vmem,) * 5,
        scratch_shapes=[pltpu.VMEM(shape, dtype) for shape, dtype in shapes]
        + [
            pltpu.SemaphoreType.DMA((COPIES,)),
            pltpu.SemaphoreType.DMA((COPIES,)),
            pltpu.SemaphoreType.DMA((5,)),
        ],
        compiler_params=pltpu.CompilerParams(
            collective_id=0, has_side_effects=True, vmem_limit_bytes=48 * 1024 * 1024
        ),
    )(
        *(
            pltpu.with_memory_space_constraint(array, pltpu.HBM)
            for array in (inputs, gain.reshape(1, FEAT), w_first, w_second, cotangent)
        )
    )
    outputs, input_grad, first_grad, second_grad, gain_grad = pl.pallas_call(
        save,
        out_shape=results,
        in_specs=[anywhere] * 5,
        out_specs=(hbm,) * 5,
        scratch_shapes=[pltpu.SemaphoreType.DMA((5,))],
    )(*made)
    return outputs, input_grad, first_grad, second_grad, gain_grad.reshape(FEAT)


def solution(mesh):
    in_specs = (
        P(None, "section", "tensor"),
        P("tensor"),
        P("tensor", "dp"),
        P("dp", "tensor"),
        P(None, ("section", "dp"), "tensor"),
    )
    out_specs = (
        P(None, ("section", "dp"), "tensor"),
        P(None, ("section", "dp"), "tensor"),
        P("tensor", "dp"),
        P("dp", "tensor"),
        P("tensor"),
    )
    return jax.shard_map(
        per_device, mesh=mesh, in_specs=in_specs, out_specs=out_specs, check_vma=False
    )
```

```python
import jax
import jax.numpy as jnp
from jax import lax
from jax.experimental import pallas as pl
from jax.experimental.pallas import tpu as pltpu
from jax.sharding import PartitionSpec as P

MESH = pl.DeviceIdType.MESH
F32 = jnp.float32
BF16 = jnp.bfloat16
D = 8192
EPSILON = 1e-06
N = 8
HID = 512
FEAT = 1024
ROW = FEAT + 256
NT = (((1,), (1,)), ((), ()))
TN = (((0,), (0,)), ((), ()))


class Phase:
    def __init__(self, make, first, last, sems, whole=None):
        self.make, self.first, self.last, self.sems, self.whole = make, first, last, sems, whole
        self.place = sems["used"]
        sems["used"] += 1

    def describe(self, src, dst, device):
        return pltpu.make_async_remote_copy(
            src_ref=src,
            dst_ref=dst,
            send_sem=self.sems["send"].at[self.send_place],
            recv_sem=self.sems["recv"].at[self.place],
            device_id=device,
            device_id_type=MESH,
        )

    def start(self):
        order = self.sems["phases"]
        self.send_place = len(order) % SENDS
        if len(order) >= SENDS:
            order[-SENDS].sent()
        order.append(self)
        if self.last - self.first <= 4:
            for k in range(self.first, self.last):
                self.describe(*self.make(k)).start()
            return

        def body(k, carry):
            self.describe(*self.make(k)).start()
            return carry

        lax.fori_loop(self.first, self.last, body, 0)

    def all(self):
        src, dst, device = self.make(self.first)
        if self.whole is not None:
            src = dst = self.whole
        return self.describe(src, dst, device)

    def arrived(self):
        self.all().wait_recv()

    def sent(self):
        self.all().wait_send()


SENDS = 16
PHASES = 40


def kernel(
    x_hbm, gain_hbm, w1_hbm, w2_hbm, cot_hbm,
    out_ref, ing_ref, first_out, second_out, gg_ref,
    x_in, gain_ref, w1, w2, cot_ref, xp, u, u_o, cg, cg_o,
    s_a, r_a, s_sq, r_sq, s_c, r_c, hid, hid_o, q, q_o, p_own, slope, scl,
    branch, r_fs, s_fz, r_fz, s_fx, r_fx,
    big, r_gs, s_gz, r_gz, s_gx, r_gx,
    e_s, e_r, gg_own, gg_r1, gg_chip, gg_rz, gg_line, gg_rx,
    send_sems, recv_sems, local_sems,
):
    s = lax.axis_index("section")
    d = lax.axis_index("dp")
    t = lax.axis_index("tensor")
    xh = d // 16
    z = lax.rem(d // 2, N)
    c = lax.rem(d, 2)

    def y_peer(k):
        return {"section": s, "dp": d, "tensor": lax.rem(t + k, N)}

    def z_place(k):
        return lax.rem(z + k, N)

    def z_peer(k):
        return {"section": s, "dp": xh * 16 + z_place(k) * 2 + c, "tensor": t}

    xh_peer = {"section": s, "dp": lax.rem(d + 16, 32), "tensor": t}
    sib_peer = {"section": s, "dp": d + 1 - 2 * c, "tensor": t}
    lo_peer = {"section": 1 - s, "dp": d, "tensor": t}
    far_peer = {"section": 1 - s, "dp": lax.rem(d + 16, 32), "tensor": t}

    sems = {"used": 0, "send": send_sems, "recv": recv_sems, "phases": []}

    load_cot = pltpu.make_async_copy(cot_hbm, cot_ref, local_sems.at[0])
    load_gain = pltpu.make_async_copy(gain_hbm, gain_ref, local_sems.at[1])
    load_x = pltpu.make_async_copy(x_hbm, x_in, local_sems.at[2])
    load_w1 = pltpu.make_async_copy(w1_hbm, w1, local_sems.at[3])
    load_w2 = pltpu.make_async_copy(w2_hbm, w2, local_sems.at[4])
    for load in (load_cot, load_gain, load_x, load_w1, load_w2):
        load.start()

    barrier = pltpu.get_barrier_semaphore()

    def greet(k, carry):
        pl.semaphore_signal(barrier, inc=1, device_id=y_peer(k), device_id_type=MESH)
        pl.semaphore_signal(barrier, inc=1, device_id=z_peer(k), device_id_type=MESH)
        return carry

    lax.fori_loop(1, N, greet, 0)
    for peer in (xh_peer, sib_peer, lo_peer, far_peer):
        pl.semaphore_signal(barrier, inc=1, device_id=peer, device_id_type=MESH)

    def y_rows(k):
        return pl.ds(pl.multiple_of(16 * lax.rem(t + k, N), 16), 16)

    my_rows = y_rows(0)
    mine = 16 + c * 8 + z
    other = c * 8 + z

    load_cot.wait()
    cot_own = jnp.concatenate([cot_ref[0].astype(F32), cot_ref[1].astype(F32)], axis=0)
    cg[mine] = cot_own.astype(BF16)

    pl.semaphore_wait(barrier, 2 * (N - 1) + 4)

    to_xh = Phase(lambda k: (cg.at[mine], cg.at[other], xh_peer), 0, 1, sems)
    to_xh.start()
    to_z = Phase(lambda k: (cg.at[mine], cg.at[mine], z_peer(k)), 1, N, sems, cg.at[pl.ds(0, N - 1)])
    to_z.start()

    row = lax.broadcasted_iota(jnp.int32, (256, 256), 0)
    col = lax.broadcasted_iota(jnp.int32, (256, 256), 1)
    x_half = jnp.where(row // 128 == 1, xh, 1 - xh)
    owner = x_half * 16 + (lax.rem(row, 64) // 8) * 2 + lax.rem(row, 128) // 64
    token = (lax.rem(row, 8) // 4) * 128 + owner * 4 + lax.rem(row, 4)
    perm = jnp.where(col == token, 1.0, 0.0).astype(BF16)
    load_x.wait()
    x_flat = x_in[...].reshape(256, FEAT)
    xs = jnp.dot(perm, x_flat, preferred_element_type=F32)
    xp[...] = xs
    load_gain.wait()
    gain = gain_ref[...]
    u[...] = (xs * gain).astype(BF16).reshape(2, 128, FEAT)
    load_w1.wait()
    s_a[...] = (
        jnp.dot(u[...].reshape(256, FEAT), w1[...], preferred_element_type=F32)
        .astype(BF16)
        .reshape(2, 128, HID)
    )
    a_y = Phase(lambda k: (s_a.at[:, y_rows(k)], r_a.at[k], y_peer(k)), 1, N, sems, r_a.at[pl.ds(1, N - 1)])
    a_y.start()

    ones = jnp.ones((8, FEAT), BF16)
    squares = []
    for h in range(2):
        rows = xp[h * 128 : (h + 1) * 128, :]
        sq = rows * rows
        hi = sq.astype(BF16)
        lo = (sq - hi.astype(F32)).astype(BF16)
        squares.append(
            lax.dot_general(ones, hi, NT, preferred_element_type=F32)
            + lax.dot_general(ones, lo, NT, preferred_element_type=F32)
        )
    place = lax.broadcasted_iota(jnp.int32, (8, 128), 0)
    s_sq[...] = jnp.where(place == 0, squares[0], squares[1])
    sq_y = Phase(lambda k: (s_sq, r_sq.at[k], y_peer(k)), 1, N, sems, r_sq.at[pl.ds(1, N - 1)])
    sq_y.start()

    to_xh.arrived()
    to_z2 = Phase(lambda k: (cg.at[other], cg.at[other], z_peer(k)), 1, N, sems, cg.at[pl.ds(0, N - 1)])
    to_z2.start()
    core_rows = pl.ds(pl.multiple_of(64 * c, 64), 64)
    u_lo = Phase(lambda k: (u.at[:, core_rows], u_o.at[:, core_rows], lo_peer), 0, 1, sems)
    u_lo.start()

    def pieces(h):
        return pl.ds(h * 16 + c * 8, 8)

    def gathered(h):
        return Phase(lambda k: (cg.at[pieces(h)], cg.at[pieces(h)], sib_peer), 0, 1, sems)

    def crossed(h):
        return Phase(lambda k: (cg.at[pieces(h)], cg_o.at[pieces(h)], lo_peer), 0, 1, sems)

    def rows_of(pieces_ref, h):
        return pieces_ref[h * 16 : (h + 1) * 16].astype(F32).reshape(128, FEAT).astype(BF16)

    c_y = [
        Phase(
            lambda k, h=h: (s_c.at[h, y_rows(k)], r_c.at[h, k], y_peer(k)),
            1,
            N,
            sems,
            r_c.at[h, pl.ds(1, N - 1)],
        )
        for h in range(2)
    ]

    def send_c(h):
        s_c[h] = lax.dot_general(
            rows_of(cg, h), w2[...], NT, preferred_element_type=F32
        ).astype(BF16)
        c_y[h].start()

    load_w2.wait()
    to_z.arrived()
    cot_sib1 = gathered(1)
    cot_sib1.start()
    cot_sib1.arrived()
    send_c(1)
    cot_lo1 = crossed(1)
    cot_lo1.start()

    sq_y.arrived()
    total_sq = s_sq[...]
    for k in range(1, N):
        total_sq = total_sq + r_sq[k]
    lane = lax.broadcasted_iota(jnp.int32, (16, 128), 1)
    spot = lax.broadcasted_iota(jnp.int32, (16, 128), 0) + 16 * t
    a_y.arrived()
    for h in range(2):
        picked = jnp.where(lane == spot, jnp.broadcast_to(total_sq[h : h + 1, :], (16, 128)), 0.0)
        scale = lax.rsqrt(jnp.sum(picked, axis=1, keepdims=True) / D + EPSILON)
        sums = s_a[h, my_rows].astype(F32)
        for k in range(1, N):
            sums = sums + r_a[k, h].astype(F32)
        pre = sums * scale
        sig = jax.nn.sigmoid(pre)
        hid[h, my_rows] = (pre * sig).astype(BF16)
        p_own[h] = sums
        slope[h] = sig * (1.0 + pre * (1.0 - sig))
        scl[h] = jnp.broadcast_to(scale, (16, 128))

    b_near = Phase(
        lambda k: (hid.at[:, my_rows], hid.at[:, my_rows], y_peer(1 + 6 * k)),
        0,
        2,
        sems,
        hid.at[:, pl.ds(0, 32)],
    )
    b_near.start()

    to_z2.arrived()
    cot_sib0 = gathered(0)
    cot_sib0.start()
    cot_sib0.arrived()
    send_c(0)
    cot_lo0 = crossed(0)
    cot_lo0.start()

    b_near.arrived()

    def pass_on(k):
        side, step = k // 2, k % 2 + 1
        rows = y_rows(1 if side else N - 1)
        return hid.at[:, rows], hid.at[:, rows], y_peer(N - step if side else step)

    def pass_far(k):
        rows = y_rows(1 if k else N - 1)
        return hid.at[k, rows], hid.at[k, rows], y_peer(N - 3 if k else 3)

    b_rest = (
        Phase(pass_far, 0, 2, sems, hid.at[0, pl.ds(0, 32)]),
        Phase(pass_on, 0, 4, sems, hid.at[:, pl.ds(0, 64)]),
    )
    for phase in b_rest:
        phase.start()

    d_y = [
        Phase(
            lambda k, h=h: (q.at[h, my_rows], q.at[h, my_rows], y_peer(k)),
            1,
            N,
            sems,
            q.at[h, pl.ds(0, 16 * (N - 1))],
        )
        for h in range(2)
    ]
    for h in (1, 0):
        c_y[h].arrived()
        sums = s_c[h, my_rows].astype(F32)
        for k in range(1, N):
            sums = sums + r_c[h, k].astype(F32)
        scale = scl[h][:, :1]
        own = sums * slope[h] * scale
        q[h, my_rows] = own.astype(BF16)
        if h == 0:
            d_y[0].start()
            d_y[1].start()
        inner = jnp.sum(own * p_own[h], axis=1, keepdims=True) * (scale * scale / D)
        e_s[:, h * 128 : (h + 1) * 128] = jnp.sum(
            jnp.where(lane == spot, inner, 0.0), axis=0, keepdims=True
        )
    e_y = Phase(lambda k: (e_s, e_r.at[k], y_peer(k)), 1, N, sems, e_r.at[pl.ds(1, N - 1)])
    e_y.start()

    for phase in b_rest:
        phase.arrived()
    hid_lo = Phase(lambda k: (hid, hid_o, lo_peer), 0, 1, sems)
    hid_lo.start()
    branch[...] = jnp.dot(
        hid[...].reshape(256, HID), w2[...], preferred_element_type=F32
    ).reshape(2, 128, FEAT)
    sib_rows = pl.ds(pl.multiple_of(64 - 64 * c, 64), 64)
    f_sib = Phase(lambda k: (branch.at[:, sib_rows], r_fs, sib_peer), 0, 1, sems)
    f_sib.start()

    u_lo.arrived()
    u_sib = Phase(lambda k: (u_o.at[:, core_rows], u_o.at[:, core_rows], sib_peer), 0, 1, sems)
    u_sib.start()

    f_sib.arrived()
    for h in range(2):
        both = branch[h, core_rows] + r_fs[h]
        s_fz[h] = both.reshape(N, 8, FEAT).astype(BF16)
    f_z = Phase(
        lambda k: (s_fz.at[:, z_place(k)], r_fz.at[k], z_peer(k)),
        1,
        N,
        sems,
        r_fz.at[pl.ds(1, N - 1)],
    )
    f_z.start()

    g_sibs = [
        Phase(lambda k, h=h: (big.at[h, sib_rows], r_gs.at[h], sib_peer), 0, 1, sems)
        for h in range(2)
    ]
    g_zs = [
        Phase(
            lambda k, h=h: (s_gz.at[h, z_place(k)], r_gz.at[h, k], z_peer(k)),
            1,
            N,
            sems,
            r_gz.at[h, pl.ds(1, N - 1)],
        )
        for h in range(2)
    ]
    q_lo = [
        Phase(lambda k, h=h: (q.at[h], q_o.at[h], lo_peer), 0, 1, sems)
        for h in range(2)
    ]
    gain_part = jnp.zeros((1, FEAT), F32)
    for h in range(2):
        d_y[h].arrived()
        part = lax.dot_general(q[h], w1[...], NT, preferred_element_type=F32)
        big[h] = part
        g_sibs[h].start()
        q_lo[h].start()
        gain_part = gain_part + jnp.sum(
            part * xp[h * 128 : (h + 1) * 128, :], axis=0, keepdims=True
        )
        if h == 1:
            e_y.arrived()
            e_sum = e_s[...]
            for k in range(1, N):
                e_sum = e_sum + e_r[k]
            gg_own[:, 0:FEAT] = gain_part
            gg_own[:, FEAT:ROW] = e_sum
            gg_sib = Phase(lambda k: (gg_own, gg_r1, sib_peer), 0, 1, sems)
            gg_sib.start()
        g_sibs[h].arrived()
        both = big[h, core_rows] + r_gs[h]
        s_gz[h] = both.reshape(N, 8, FEAT).astype(BF16)
        g_zs[h].start()
    gg_sib.arrived()
    gg_chip[...] = gg_own[...] + gg_r1[...]
    gg_z = Phase(lambda k: (gg_chip, gg_rz.at[k], z_peer(k)), 1, N, sems, gg_rz.at[pl.ds(1, N - 1)])
    gg_z.start()

    cot_sibo = [
        Phase(lambda k, h=h: (cg_o.at[pieces(h)], cg_o.at[pieces(h)], sib_peer), 0, 1, sems)
        for h in range(2)
    ]
    cot_lo1.arrived()
    cot_sibo[1].start()
    cot_lo0.arrived()
    cot_sibo[0].start()
    hid_lo.arrived()
    for h in range(2):
        cot_sibo[h].arrived()
    hid_all = jnp.concatenate(
        [hid[...].reshape(256, HID), hid_o[...].reshape(256, HID)], axis=0
    )
    cot_all = jnp.concatenate(
        [rows_of(cg, 0), rows_of(cg, 1), rows_of(cg_o, 0), rows_of(cg_o, 1)], axis=0
    )
    second_out[...] = lax.dot_general(
        hid_all, cot_all, TN, preferred_element_type=F32
    ).astype(BF16)

    def z_total(sent, received, h):
        total = sent[h, z].astype(F32)
        for k in range(1, N):
            total = total + received(k)
        return total

    f_z.arrived()
    s_fx[...] = z_total(s_fz, lambda k: r_fz[k, 0].astype(F32), 0)
    f_xh = Phase(lambda k: (s_fx, r_fx, xh_peer), 0, 1, sems)
    f_xh.start()
    own_branch = z_total(s_fz, lambda k: r_fz[k, 1].astype(F32), 1)

    g_zs[0].arrived()
    s_gx[...] = z_total(s_gz, lambda k: r_gz[0, k].astype(F32), 0)
    g_xh = Phase(lambda k: (s_gx, r_gx, xh_peer), 0, 1, sems)
    g_xh.start()

    gg_z.arrived()
    gg_total = gg_chip[...]
    for k in range(1, N):
        gg_total = gg_total + gg_rz[k]
    gg_line[...] = gg_total
    x_peers = (xh_peer, lo_peer, far_peer)
    gg_x = Phase(lambda k: (gg_line, gg_rx.at[k], x_peers[k]), 0, 3, sems, gg_rx)
    gg_x.start()

    u_sib.arrived()
    for h in range(2):
        q_lo[h].arrived()
    u_all = jnp.concatenate([u[...].reshape(256, FEAT), u_o[...].reshape(256, FEAT)], axis=0)
    q_all = jnp.concatenate(
        [q[...].reshape(256, HID), q_o[...].reshape(256, HID)], axis=0
    )
    first_out[...] = lax.dot_general(u_all, q_all, TN, preferred_element_type=F32).astype(BF16)

    x_own = xp[pl.ds(pl.multiple_of(mine * 8, 8), 8), :]
    f_xh.arrived()
    outputs = x_own + own_branch + r_fx[...]
    out_ref[0] = outputs[0:4].astype(BF16)
    out_ref[1] = outputs[4:8].astype(BF16)

    g_zs[1].arrived()
    normed_grad = z_total(s_gz, lambda k: r_gz[1, k].astype(F32), 1)
    g_xh.arrived()
    normed_grad = normed_grad + r_gx[...]
    gg_x.arrived()
    inner_row = gg_line[:, FEAT + 128 : ROW] + gg_rx[0][:, FEAT : FEAT + 128]
    own_lane = lax.broadcasted_iota(jnp.int32, (8, 128), 1)
    own_spot = lax.broadcasted_iota(jnp.int32, (8, 128), 0) + c * 64 + z * 8
    inner = jnp.sum(
        jnp.where(own_lane == own_spot, jnp.broadcast_to(inner_row, (8, 128)), 0.0),
        axis=1,
        keepdims=True,
    )
    grads = cg[mine].astype(F32) + gain * normed_grad - x_own * inner
    ing_ref[0] = grads[0:4].astype(BF16)
    ing_ref[1] = grads[4:8].astype(BF16)
    gg_ref[...] = (gg_line[:, 0:FEAT] + gg_rx[0][:, 0:FEAT]) + (
        gg_rx[1][:, 0:FEAT] + gg_rx[2][:, 0:FEAT]
    )

    for phase in sems["phases"][-SENDS:]:
        phase.sent()


def save(*refs):
    sources, targets, sems = refs[:5], refs[5:10], refs[10]
    copies = [pltpu.make_async_copy(sources[i], targets[i], sems.at[i]) for i in range(5)]
    for copy in copies:
        copy.start()
    for copy in copies:
        copy.wait()


def per_device(inputs, gain, w_first, w_second, cotangent):
    vmem = pl.BlockSpec(memory_space=pltpu.VMEM)
    hbm = pl.BlockSpec(memory_space=pltpu.HBM)
    anywhere = pl.BlockSpec(memory_space=pl.ANY)
    shapes = [
        ((2, 128, FEAT), BF16),
        ((1, FEAT), F32),
        ((FEAT, HID), BF16),
        ((HID, FEAT), BF16),
        ((2, 4, FEAT), BF16),
        ((256, FEAT), F32),
        ((2, 128, FEAT), BF16),
        ((2, 128, FEAT), BF16),
        ((32, 8, FEAT), BF16),
        ((32, 8, FEAT), BF16),
        ((2, 128, HID), BF16),
        ((N, 2, 16, HID), BF16),
        ((8, 128), F32),
        ((N, 8, 128), F32),
        ((2, 128, HID), BF16),
        ((2, N, 16, HID), BF16),
        ((2, 128, HID), BF16),
        ((2, 128, HID), BF16),
        ((2, 128, HID), BF16),
        ((2, 128, HID), BF16),
        ((2, 16, HID), F32),
        ((2, 16, HID), F32),
        ((2, 16, 128), F32),
        ((2, 128, FEAT), F32),
        ((2, 64, FEAT), F32),
        ((2, N, 8, FEAT), BF16),
        ((N, 2, 8, FEAT), BF16),
        ((8, FEAT), F32),
        ((8, FEAT), F32),
        ((2, 128, FEAT), F32),
        ((2, 64, FEAT), F32),
        ((2, N, 8, FEAT), BF16),
        ((2, N, 8, FEAT), BF16),
        ((8, FEAT), F32),
        ((8, FEAT), F32),
        ((1, 256), F32),
        ((N, 1, 256), F32),
        ((1, ROW), F32),
        ((1, ROW), F32),
        ((1, ROW), F32),
        ((N, 1, ROW), F32),
        ((1, ROW), F32),
        ((3, 1, ROW), F32),
    ]
    results = (
        jax.ShapeDtypeStruct(cotangent.shape, BF16),
        jax.ShapeDtypeStruct(cotangent.shape, BF16),
        jax.ShapeDtypeStruct(w_first.shape, BF16),
        jax.ShapeDtypeStruct(w_second.shape, BF16),
        jax.ShapeDtypeStruct((1, FEAT), F32),
    )
    made = pl.pallas_call(
        kernel,
        out_shape=results,
        in_specs=[hbm] * 5,
        out_specs=(vmem,) * 5,
        scratch_shapes=[pltpu.VMEM(shape, dtype) for shape, dtype in shapes]
        + [
            pltpu.SemaphoreType.DMA((SENDS,)),
            pltpu.SemaphoreType.DMA((PHASES,)),
            pltpu.SemaphoreType.DMA((5,)),
        ],
        compiler_params=pltpu.CompilerParams(
            collective_id=0, has_side_effects=True, vmem_limit_bytes=48 * 1024 * 1024
        ),
    )(
        *(
            pltpu.with_memory_space_constraint(array, pltpu.HBM)
            for array in (inputs, gain.reshape(1, FEAT), w_first, w_second, cotangent)
        )
    )
    outputs, input_grad, first_grad, second_grad, gain_grad = pl.pallas_call(
        save,
        out_shape=results,
        in_specs=[vmem] * 5,
        out_specs=(anywhere,) * 5,
        scratch_shapes=[pltpu.SemaphoreType.DMA((5,))],
    )(*made)
    return outputs, input_grad, first_grad, second_grad, gain_grad.reshape(FEAT)


def solution(mesh):
    in_specs = (
        P(None, "section", "tensor"),
        P("tensor"),
        P("tensor", "dp"),
        P("dp", "tensor"),
        P(None, ("section", "dp"), "tensor"),
    )
    out_specs = (
        P(None, ("section", "dp"), "tensor"),
        P(None, ("section", "dp"), "tensor"),
        P("tensor", "dp"),
        P("dp", "tensor"),
        P("tensor"),
    )
    return jax.shard_map(
        per_device, mesh=mesh, in_specs=in_specs, out_specs=out_specs, check_vma=False
    )
```

```python
import jax
import jax.numpy as jnp
from jax import lax
from jax.experimental import pallas as pl
from jax.experimental.pallas import tpu as pltpu
from jax.sharding import PartitionSpec as P

MESH = pl.DeviceIdType.MESH
F32 = jnp.float32
BF16 = jnp.bfloat16
D = 8192
EPSILON = 1e-06
N = 8
HID = 512
FEAT = 1024
ROW = FEAT + 256
NT = (((1,), (1,)), ((), ()))
TN = (((0,), (0,)), ((), ()))


class Phase:
    def __init__(self, make, first, last, sems, whole=None):
        self.make, self.first, self.last, self.sems, self.whole = make, first, last, sems, whole
        self.place = sems["used"]
        sems["used"] += 1

    def describe(self, src, dst, device):
        return pltpu.make_async_remote_copy(
            src_ref=src,
            dst_ref=dst,
            send_sem=self.sems["send"].at[self.send_place],
            recv_sem=self.sems["recv"].at[self.place],
            device_id=device,
            device_id_type=MESH,
        )

    def start(self):
        order = self.sems["phases"]
        self.send_place = len(order) % SENDS
        if len(order) >= SENDS:
            order[-SENDS].sent()
        order.append(self)
        if self.last - self.first <= 4:
            for k in range(self.first, self.last):
                self.describe(*self.make(k)).start()
            return

        def body(k, carry):
            self.describe(*self.make(k)).start()
            return carry

        lax.fori_loop(self.first, self.last, body, 0)

    def all(self):
        src, dst, device = self.make(self.first)
        if self.whole is not None:
            src = dst = self.whole
        return self.describe(src, dst, device)

    def arrived(self):
        self.all().wait_recv()

    def sent(self):
        self.all().wait_send()


SENDS = 16
FAR = (1, N - 1, 3, N - 3)
PHASES = 37


def kernel(
    x_hbm, gain_hbm, w1_hbm, w2_hbm, cot_hbm,
    out_ref, ing_ref, first_out, second_out, gg_ref,
    x_in, gain_ref, w1, w2, cot_ref, xp, u, u_o, cg, cg_o,
    s_a, r_a, s_sq, r_sq, s_c, r_c, hid, hid_o, q, q_o, p_own, slope, scl,
    branch, r_fs, s_fz, r_fz, r_ff, r_f2, s_fx, r_fx,
    big, r_gs, s_gz, r_gz, s_gx, r_gx,
    e_s, e_r, gg_own, gg_r1, gg_chip, gg_rz, gg_line, gg_rx,
    send_sems, recv_sems, local_sems,
):
    s = lax.axis_index("section")
    d = lax.axis_index("dp")
    t = lax.axis_index("tensor")
    xh = d // 16
    z = lax.rem(d // 2, N)
    c = lax.rem(d, 2)

    def y_peer(k):
        return {"section": s, "dp": d, "tensor": lax.rem(t + k, N)}

    def z_place(k):
        return lax.rem(z + k, N)

    def z_peer(k):
        return {"section": s, "dp": xh * 16 + z_place(k) * 2 + c, "tensor": t}

    xh_peer = {"section": s, "dp": lax.rem(d + 16, 32), "tensor": t}
    sib_peer = {"section": s, "dp": d + 1 - 2 * c, "tensor": t}
    lo_peer = {"section": 1 - s, "dp": d, "tensor": t}
    far_peer = {"section": 1 - s, "dp": lax.rem(d + 16, 32), "tensor": t}

    sems = {"used": 0, "send": send_sems, "recv": recv_sems, "phases": []}

    load_cot = pltpu.make_async_copy(cot_hbm, cot_ref, local_sems.at[0])
    load_gain = pltpu.make_async_copy(gain_hbm, gain_ref, local_sems.at[1])
    load_x = pltpu.make_async_copy(x_hbm, x_in, local_sems.at[2])
    load_w1 = pltpu.make_async_copy(w1_hbm, w1, local_sems.at[3])
    load_w2 = pltpu.make_async_copy(w2_hbm, w2, local_sems.at[4])
    for load in (load_cot, load_gain, load_x, load_w1, load_w2):
        load.start()

    barrier = pltpu.get_barrier_semaphore()

    def greet(k, carry):
        pl.semaphore_signal(barrier, inc=1, device_id=y_peer(k), device_id_type=MESH)
        pl.semaphore_signal(barrier, inc=1, device_id=z_peer(k), device_id_type=MESH)
        return carry

    lax.fori_loop(1, N, greet, 0)
    for peer in (xh_peer, sib_peer, lo_peer, far_peer):
        pl.semaphore_signal(barrier, inc=1, device_id=peer, device_id_type=MESH)

    def y_rows(k):
        return pl.ds(pl.multiple_of(16 * lax.rem(t + k, N), 16), 16)

    my_rows = y_rows(0)
    mine = 16 + c * 8 + z
    other = c * 8 + z

    load_cot.wait()
    cot_own = jnp.concatenate([cot_ref[0].astype(F32), cot_ref[1].astype(F32)], axis=0)
    cg[mine] = cot_own.astype(BF16)

    row = lax.broadcasted_iota(jnp.int32, (256, 256), 0)
    col = lax.broadcasted_iota(jnp.int32, (256, 256), 1)
    x_half = jnp.where(row // 128 == 1, xh, 1 - xh)
    owner = x_half * 16 + (lax.rem(row, 64) // 8) * 2 + lax.rem(row, 128) // 64
    token = (lax.rem(row, 8) // 4) * 128 + owner * 4 + lax.rem(row, 4)
    perm = jnp.where(col == token, 1.0, 0.0).astype(BF16)
    load_x.wait()
    x_flat = x_in[...].reshape(256, FEAT)
    xs = jnp.dot(perm, x_flat, preferred_element_type=F32)
    xp[...] = xs
    load_gain.wait()
    gain = gain_ref[...]
    u[...] = (xs * gain).astype(BF16).reshape(2, 128, FEAT)
    load_w1.wait()
    s_a[...] = (
        jnp.dot(u[...].reshape(256, FEAT), w1[...], preferred_element_type=F32)
        .astype(BF16)
        .reshape(2, 128, HID)
    )
    pl.semaphore_wait(barrier, 2 * (N - 1) + 4)
    a_y = Phase(lambda k: (s_a.at[:, y_rows(k)], r_a.at[k], y_peer(k)), 1, N, sems, r_a.at[pl.ds(1, N - 1)])
    a_y.start()
    to_xh = Phase(lambda k: (cg.at[mine], cg.at[other], xh_peer), 0, 1, sems)
    to_xh.start()
    to_z = Phase(lambda k: (cg.at[mine], cg.at[mine], z_peer(k)), 1, N, sems, cg.at[pl.ds(0, N - 1)])
    to_z.start()

    ones = jnp.ones((8, FEAT), BF16)
    squares = []
    for h in range(2):
        rows = xp[h * 128 : (h + 1) * 128, :]
        sq = rows * rows
        hi = sq.astype(BF16)
        lo = (sq - hi.astype(F32)).astype(BF16)
        squares.append(
            lax.dot_general(ones, hi, NT, preferred_element_type=F32)
            + lax.dot_general(ones, lo, NT, preferred_element_type=F32)
        )
    place = lax.broadcasted_iota(jnp.int32, (8, 128), 0)
    s_sq[...] = jnp.where(place == 0, squares[0], squares[1])
    sq_y = Phase(lambda k: (s_sq, r_sq.at[k], y_peer(k)), 1, N, sems, r_sq.at[pl.ds(1, N - 1)])
    sq_y.start()

    to_xh.arrived()
    to_z2 = Phase(lambda k: (cg.at[other], cg.at[other], z_peer(k)), 1, N, sems, cg.at[pl.ds(0, N - 1)])
    to_z2.start()
    core_rows = pl.ds(pl.multiple_of(64 * c, 64), 64)
    u_lo = Phase(lambda k: (u.at[:, core_rows], u_o.at[:, core_rows], lo_peer), 0, 1, sems)
    u_lo.start()

    def pieces(h):
        return pl.ds(h * 16 + c * 8, 8)

    def gathered(h):
        return Phase(lambda k: (cg.at[pieces(h)], cg.at[pieces(h)], sib_peer), 0, 1, sems)

    def crossed(h):
        return Phase(lambda k: (cg.at[pieces(h)], cg_o.at[pieces(h)], lo_peer), 0, 1, sems)

    def rows_of(pieces_ref, h):
        return pieces_ref[h * 16 : (h + 1) * 16].astype(F32).reshape(128, FEAT).astype(BF16)

    c_y = [
        Phase(
            lambda k, h=h: (s_c.at[h, y_rows(k)], r_c.at[h, k], y_peer(k)),
            1,
            N,
            sems,
            r_c.at[h, pl.ds(1, N - 1)],
        )
        for h in range(2)
    ]

    def send_c(h):
        s_c[h] = lax.dot_general(
            rows_of(cg, h), w2[...], NT, preferred_element_type=F32
        ).astype(BF16)
        c_y[h].start()

    load_w2.wait()
    to_z.arrived()
    cot_sib1 = gathered(1)
    cot_sib1.start()
    cot_sib1.arrived()
    send_c(1)
    cot_lo1 = crossed(1)
    cot_lo1.start()

    sq_y.arrived()
    total_sq = s_sq[...]
    for k in range(1, N):
        total_sq = total_sq + r_sq[k]
    lane = lax.broadcasted_iota(jnp.int32, (16, 128), 1)
    spot = lax.broadcasted_iota(jnp.int32, (16, 128), 0) + 16 * t
    a_y.arrived()
    for h in range(2):
        picked = jnp.where(lane == spot, jnp.broadcast_to(total_sq[h : h + 1, :], (16, 128)), 0.0)
        scale = lax.rsqrt(jnp.sum(picked, axis=1, keepdims=True) / D + EPSILON)
        sums = s_a[h, my_rows].astype(F32)
        for k in range(1, N):
            sums = sums + r_a[k, h].astype(F32)
        pre = sums * scale
        sig = jax.nn.sigmoid(pre)
        hid[h, my_rows] = (pre * sig).astype(BF16)
        p_own[h] = sums
        slope[h] = sig * (1.0 + pre * (1.0 - sig))
        scl[h] = jnp.broadcast_to(scale, (16, 128))

    b_near = Phase(
        lambda k: (hid.at[:, my_rows], hid.at[:, my_rows], y_peer(1 + 6 * k)),
        0,
        2,
        sems,
        hid.at[:, pl.ds(0, 32)],
    )
    b_near.start()

    to_z2.arrived()
    cot_sib0 = gathered(0)
    cot_sib0.start()
    cot_sib0.arrived()
    send_c(0)
    cot_lo0 = crossed(0)
    cot_lo0.start()

    b_near.arrived()

    def pass_on(k):
        side, step = k // 2, k % 2 + 1
        rows = y_rows(1 if side else N - 1)
        return hid.at[:, rows], hid.at[:, rows], y_peer(N - step if side else step)

    def pass_far(k):
        rows = y_rows(1 if k else N - 1)
        return hid.at[k, rows], hid.at[k, rows], y_peer(N - 3 if k else 3)

    b_rest = (
        Phase(pass_far, 0, 2, sems, hid.at[0, pl.ds(0, 32)]),
        Phase(pass_on, 0, 4, sems, hid.at[:, pl.ds(0, 64)]),
    )
    for phase in b_rest:
        phase.start()

    d_y = [
        Phase(
            lambda k, h=h: (q.at[h, my_rows], q.at[h, my_rows], y_peer(k)),
            1,
            N,
            sems,
            q.at[h, pl.ds(0, 16 * (N - 1))],
        )
        for h in range(2)
    ]
    for h in (1, 0):
        c_y[h].arrived()
        sums = s_c[h, my_rows].astype(F32)
        for k in range(1, N):
            sums = sums + r_c[h, k].astype(F32)
        scale = scl[h][:, :1]
        own = sums * slope[h] * scale
        q[h, my_rows] = own.astype(BF16)
        if h == 0:
            d_y[0].start()
            d_y[1].start()
        inner = jnp.sum(own * p_own[h], axis=1, keepdims=True) * (scale * scale / D)
        e_s[:, h * 128 : (h + 1) * 128] = jnp.sum(
            jnp.where(lane == spot, inner, 0.0), axis=0, keepdims=True
        )
    e_y = Phase(lambda k: (e_s, e_r.at[k], y_peer(k)), 1, N, sems, e_r.at[pl.ds(1, N - 1)])
    e_y.start()

    for phase in b_rest:
        phase.arrived()
    hid_lo = Phase(lambda k: (hid, hid_o, lo_peer), 0, 1, sems)
    hid_lo.start()
    branch[...] = jnp.dot(
        hid[...].reshape(256, HID), w2[...], preferred_element_type=F32
    ).reshape(2, 128, FEAT)
    sib_rows = pl.ds(pl.multiple_of(64 - 64 * c, 64), 64)
    f_sib = Phase(lambda k: (branch.at[:, sib_rows], r_fs, sib_peer), 0, 1, sems)
    f_sib.start()

    u_lo.arrived()
    u_sib = Phase(lambda k: (u_o.at[:, core_rows], u_o.at[:, core_rows], sib_peer), 0, 1, sems)
    u_sib.start()

    f_sib.arrived()
    for h in range(2):
        both = branch[h, core_rows] + r_fs[h]
        s_fz[h] = both.reshape(N, 8, FEAT).astype(BF16)

    def f_near(k):
        step = N - 1 if k % 2 else 1
        if k < 2:
            return s_fz.at[:, z_place(2 * step)], r_fz.at[k], z_peer(step)
        return s_fz.at[k - 2, z_place(4)], r_ff.at[k - 2], z_peer(step)

    f_one = Phase(f_near, 0, 2, sems, r_fz)
    f_one.start()
    f_four = Phase(lambda k: f_near(k + 2), 0, 2, sems, r_ff)
    f_four.start()

    g_sibs = [
        Phase(lambda k, h=h: (big.at[h, sib_rows], r_gs.at[h], sib_peer), 0, 1, sems)
        for h in range(2)
    ]
    g_zs = [
        Phase(
            lambda k, h=h: (s_gz.at[h, z_place(k)], r_gz.at[h, k], z_peer(k)),
            1,
            N,
            sems,
            r_gz.at[h, pl.ds(1, N - 1)],
        )
        for h in range(2)
    ]
    q_lo = [
        Phase(lambda k, h=h: (q.at[h], q_o.at[h], lo_peer), 0, 1, sems)
        for h in range(2)
    ]
    f_far = Phase(
        lambda k: (s_fz.at[:, z_place(FAR[k])], r_f2.at[k], z_peer(FAR[k])), 0, 4, sems, r_f2
    )

    def pass_f():
        f_one.arrived()
        f_four.arrived()
        for k, step in ((0, 1), (1, N - 1)):
            to = z_place(step)
            for h in range(2):
                s_fz[h, to] = (s_fz[h, to].astype(F32) + r_fz[k, h].astype(F32)).astype(BF16)
            to = z_place(3 * step)
            s_fz[k, to] = (s_fz[k, to].astype(F32) + r_ff[k].astype(F32)).astype(BF16)
        f_far.start()

    gain_part = jnp.zeros((1, FEAT), F32)
    for h in range(2):
        d_y[h].arrived()
        for rows in (sib_rows, core_rows):
            part = lax.dot_general(q[h, rows], w1[...], NT, preferred_element_type=F32)
            big[h, rows] = part
            if rows is sib_rows:
                g_sibs[h].start()
        q_lo[h].start()
        gain_part = gain_part + jnp.sum(
            big[h] * xp[h * 128 : (h + 1) * 128, :], axis=0, keepdims=True
        )
        if h == 1:
            e_y.arrived()
            e_sum = e_s[...]
            for k in range(1, N):
                e_sum = e_sum + e_r[k]
            gg_own[:, 0:FEAT] = gain_part
            gg_own[:, FEAT:ROW] = e_sum
            gg_sib = Phase(lambda k: (gg_own, gg_r1, sib_peer), 0, 1, sems)
            gg_sib.start()
        g_sibs[h].arrived()
        both = big[h, core_rows] + r_gs[h]
        s_gz[h] = both.reshape(N, 8, FEAT).astype(BF16)
        if h == 1:
            gg_sib.arrived()
            gg_chip[...] = gg_own[...] + gg_r1[...]
            gg_z = Phase(
                lambda k: (gg_chip, gg_rz.at[k], z_peer(k)), 1, N, sems, gg_rz.at[pl.ds(1, N - 1)]
            )
            gg_z.start()
        g_zs[h].start()
        if h == 0:
            pass_f()

    cot_sibo = [
        Phase(lambda k, h=h: (cg_o.at[pieces(h)], cg_o.at[pieces(h)], sib_peer), 0, 1, sems)
        for h in range(2)
    ]
    cot_lo1.arrived()
    cot_sibo[1].start()
    cot_lo0.arrived()
    cot_sibo[0].start()
    hid_lo.arrived()
    for h in range(2):
        cot_sibo[h].arrived()
    hid_all = jnp.concatenate(
        [hid[...].reshape(256, HID), hid_o[...].reshape(256, HID)], axis=0
    )
    cot_all = jnp.concatenate(
        [rows_of(cg, 0), rows_of(cg, 1), rows_of(cg_o, 0), rows_of(cg_o, 1)], axis=0
    )
    second_out[...] = lax.dot_general(
        hid_all, cot_all, TN, preferred_element_type=F32
    ).astype(BF16)

    def z_total(sent, received, h):
        total = sent[h, z].astype(F32)
        for k in range(1, N):
            total = total + received(k)
        return total

    def f_total(h):
        total = s_fz[h, z].astype(F32)
        for k in range(4):
            total = total + r_f2[k, h].astype(F32)
        return total

    f_far.arrived()
    s_fx[...] = f_total(0)
    f_xh = Phase(lambda k: (s_fx, r_fx, xh_peer), 0, 1, sems)
    f_xh.start()
    own_branch = f_total(1)

    g_zs[0].arrived()
    s_gx[...] = z_total(s_gz, lambda k: r_gz[0, k].astype(F32), 0)
    g_xh = Phase(lambda k: (s_gx, r_gx, xh_peer), 0, 1, sems)
    g_xh.start()

    gg_z.arrived()
    gg_total = gg_chip[...]
    for k in range(1, N):
        gg_total = gg_total + gg_rz[k]
    gg_line[...] = gg_total
    x_peers = (xh_peer, lo_peer, far_peer)
    gg_x = Phase(lambda k: (gg_line, gg_rx.at[k], x_peers[k]), 0, 3, sems, gg_rx)
    gg_x.start()

    u_sib.arrived()
    for h in range(2):
        q_lo[h].arrived()
    u_all = jnp.concatenate([u[...].reshape(256, FEAT), u_o[...].reshape(256, FEAT)], axis=0)
    q_all = jnp.concatenate(
        [q[...].reshape(256, HID), q_o[...].reshape(256, HID)], axis=0
    )
    first_out[...] = lax.dot_general(u_all, q_all, TN, preferred_element_type=F32).astype(BF16)

    x_own = xp[pl.ds(pl.multiple_of(mine * 8, 8), 8), :]
    f_xh.arrived()
    outputs = x_own + own_branch + r_fx[...]
    out_ref[0] = outputs[0:4].astype(BF16)
    out_ref[1] = outputs[4:8].astype(BF16)

    g_zs[1].arrived()
    normed_grad = z_total(s_gz, lambda k: r_gz[1, k].astype(F32), 1)
    g_xh.arrived()
    normed_grad = normed_grad + r_gx[...]
    gg_x.arrived()
    inner_row = gg_line[:, FEAT + 128 : ROW] + gg_rx[0][:, FEAT : FEAT + 128]
    own_lane = lax.broadcasted_iota(jnp.int32, (8, 128), 1)
    own_spot = lax.broadcasted_iota(jnp.int32, (8, 128), 0) + c * 64 + z * 8
    inner = jnp.sum(
        jnp.where(own_lane == own_spot, jnp.broadcast_to(inner_row, (8, 128)), 0.0),
        axis=1,
        keepdims=True,
    )
    grads = cg[mine].astype(F32) + gain * normed_grad - x_own * inner
    ing_ref[0] = grads[0:4].astype(BF16)
    ing_ref[1] = grads[4:8].astype(BF16)
    gg_ref[...] = (gg_line[:, 0:FEAT] + gg_rx[0][:, 0:FEAT]) + (
        gg_rx[1][:, 0:FEAT] + gg_rx[2][:, 0:FEAT]
    )

    for phase in sems["phases"][-SENDS:]:
        phase.sent()


def save(*refs):
    sources, targets, sems = refs[:5], refs[5:10], refs[10]
    copies = [pltpu.make_async_copy(sources[i], targets[i], sems.at[i]) for i in range(5)]
    for copy in copies:
        copy.start()
    for copy in copies:
        copy.wait()


def per_device(inputs, gain, w_first, w_second, cotangent):
    vmem = pl.BlockSpec(memory_space=pltpu.VMEM)
    hbm = pl.BlockSpec(memory_space=pltpu.HBM)
    anywhere = pl.BlockSpec(memory_space=pl.ANY)
    shapes = [
        ((2, 128, FEAT), BF16),
        ((1, FEAT), F32),
        ((FEAT, HID), BF16),
        ((HID, FEAT), BF16),
        ((2, 4, FEAT), BF16),
        ((256, FEAT), F32),
        ((2, 128, FEAT), BF16),
        ((2, 128, FEAT), BF16),
        ((32, 8, FEAT), BF16),
        ((32, 8, FEAT), BF16),
        ((2, 128, HID), BF16),
        ((N, 2, 16, HID), BF16),
        ((8, 128), F32),
        ((N, 8, 128), F32),
        ((2, 128, HID), BF16),
        ((2, N, 16, HID), BF16),
        ((2, 128, HID), BF16),
        ((2, 128, HID), BF16),
        ((2, 128, HID), BF16),
        ((2, 128, HID), BF16),
        ((2, 16, HID), F32),
        ((2, 16, HID), F32),
        ((2, 16, 128), F32),
        ((2, 128, FEAT), F32),
        ((2, 64, FEAT), F32),
        ((2, N, 8, FEAT), BF16),
        ((2, 2, 8, FEAT), BF16),
        ((2, 8, FEAT), BF16),
        ((4, 2, 8, FEAT), BF16),
        ((8, FEAT), F32),
        ((8, FEAT), F32),
        ((2, 128, FEAT), F32),
        ((2, 64, FEAT), F32),
        ((2, N, 8, FEAT), BF16),
        ((2, N, 8, FEAT), BF16),
        ((8, FEAT), F32),
        ((8, FEAT), F32),
        ((1, 256), F32),
        ((N, 1, 256), F32),
        ((1, ROW), F32),
        ((1, ROW), F32),
        ((1, ROW), F32),
        ((N, 1, ROW), F32),
        ((1, ROW), F32),
        ((3, 1, ROW), F32),
    ]
    results = (
        jax.ShapeDtypeStruct(cotangent.shape, BF16),
        jax.ShapeDtypeStruct(cotangent.shape, BF16),
        jax.ShapeDtypeStruct(w_first.shape, BF16),
        jax.ShapeDtypeStruct(w_second.shape, BF16),
        jax.ShapeDtypeStruct((1, FEAT), F32),
    )
    made = pl.pallas_call(
        kernel,
        out_shape=results,
        in_specs=[hbm] * 5,
        out_specs=(vmem,) * 5,
        scratch_shapes=[pltpu.VMEM(shape, dtype) for shape, dtype in shapes]
        + [
            pltpu.SemaphoreType.DMA((SENDS,)),
            pltpu.SemaphoreType.DMA((PHASES,)),
            pltpu.SemaphoreType.DMA((5,)),
        ],
        compiler_params=pltpu.CompilerParams(
            collective_id=0, has_side_effects=True, vmem_limit_bytes=48 * 1024 * 1024
        ),
    )(
        *(
            pltpu.with_memory_space_constraint(array, pltpu.HBM)
            for array in (inputs, gain.reshape(1, FEAT), w_first, w_second, cotangent)
        )
    )
    outputs, input_grad, first_grad, second_grad, gain_grad = pl.pallas_call(
        save,
        out_shape=results,
        in_specs=[vmem] * 5,
        out_specs=(anywhere,) * 5,
        scratch_shapes=[pltpu.SemaphoreType.DMA((5,))],
    )(*made)
    return outputs, input_grad, first_grad, second_grad, gain_grad.reshape(FEAT)


def solution(mesh):
    in_specs = (
        P(None, "section", "tensor"),
        P("tensor"),
        P("tensor", "dp"),
        P("dp", "tensor"),
        P(None, ("section", "dp"), "tensor"),
    )
    out_specs = (
        P(None, ("section", "dp"), "tensor"),
        P(None, ("section", "dp"), "tensor"),
        P("tensor", "dp"),
        P("dp", "tensor"),
        P("tensor"),
    )
    return jax.shard_map(
        per_device, mesh=mesh, in_specs=in_specs, out_specs=out_specs, check_vma=False
    )
```

```python
import jax
import jax.numpy as jnp
from jax import lax
from jax.experimental import pallas as pl
from jax.experimental.pallas import tpu as pltpu
from jax.sharding import PartitionSpec as P

MESH = pl.DeviceIdType.MESH
F32 = jnp.float32
BF16 = jnp.bfloat16
D = 8192
EPSILON = 1e-06
N = 8
HID = 512
FEAT = 1024
NT = (((1,), (1,)), ((), ()))
TN = (((0,), (0,)), ((), ()))


class Phase:
    def __init__(self, make, first, last, sems, whole=None):
        self.make, self.first, self.last, self.sems, self.whole = make, first, last, sems, whole
        self.place = sems["used"]
        sems["used"] += 1

    def describe(self, src, dst, device):
        return pltpu.make_async_remote_copy(
            src_ref=src,
            dst_ref=dst,
            send_sem=self.sems["send"].at[self.send_place],
            recv_sem=self.sems["recv"].at[self.place],
            device_id=device,
            device_id_type=MESH,
        )

    def start(self):
        phases = self.sems["phases"]
        self.send_place = len(phases) % SENDS
        if len(phases) >= SENDS:
            phases[-SENDS].sent()
        phases.append(self)
        order = FARTHEST_FIRST if self.last == N else range(self.first, self.last)
        for k in order:
            self.describe(*self.make(k)).start()

    def all(self):
        src, dst, device = self.make(self.first)
        if self.whole is not None:
            src = dst = self.whole
        return self.describe(src, dst, device)

    def arrived(self):
        self.all().wait_recv()

    def sent(self):
        self.all().wait_send()


SENDS = 16
FAR = (3, N - 3, 1, N - 1)
FARTHEST_FIRST = (3, 5, 4, 2, 6, 1, 7)
PHASES = 40


def kernel(
    x_hbm, gain_hbm, w1_hbm, w2_hbm, cot_hbm,
    out_ref, ing_ref, first_out, second_out, gg_ref,
    x_in, gain_ref, w1, w2, cot_ref, xp, u, u_o, cg, cg_o,
    s_a, r_a, s_sq, r_sq, s_c, r_c, hid, hid_o, q, q_o, p_own, slope, scl,
    branch, r_fs, s_fz, r_fz, r_ff, r_f2, s_fx, r_fx,
    big, r_gs, s_gz, r_gz, s_gx, r_gx,
    e_s, e_r, ee_own, ee_r1, ee_chip, ee_rz, ee_line, ee_rx, gg_own, gg_r1, gg_chip, gg_rz, gg_line, gg_rx,
    send_sems, recv_sems, local_sems,
):
    s = lax.axis_index("section")
    d = lax.axis_index("dp")
    t = lax.axis_index("tensor")
    xh = d // 16
    z = lax.rem(d // 2, N)
    c = lax.rem(d, 2)

    def y_peer(k):
        return {"section": s, "dp": d, "tensor": lax.rem(t + k, N)}

    def z_place(k):
        return lax.rem(z + k, N)

    def z_peer(k):
        return {"section": s, "dp": xh * 16 + z_place(k) * 2 + c, "tensor": t}

    xh_peer = {"section": s, "dp": lax.rem(d + 16, 32), "tensor": t}
    sib_peer = {"section": s, "dp": d + 1 - 2 * c, "tensor": t}
    lo_peer = {"section": 1 - s, "dp": d, "tensor": t}
    far_peer = {"section": 1 - s, "dp": lax.rem(d + 16, 32), "tensor": t}

    sems = {"used": 0, "send": send_sems, "recv": recv_sems, "phases": []}

    load_cot = pltpu.make_async_copy(cot_hbm, cot_ref, local_sems.at[0])
    load_gain = pltpu.make_async_copy(gain_hbm, gain_ref, local_sems.at[1])
    load_x = pltpu.make_async_copy(x_hbm, x_in, local_sems.at[2])
    load_w1 = pltpu.make_async_copy(w1_hbm, w1, local_sems.at[3])
    load_w2 = pltpu.make_async_copy(w2_hbm, w2, local_sems.at[4])
    for load in (load_cot, load_gain, load_x, load_w1, load_w2):
        load.start()

    barrier = pltpu.get_barrier_semaphore()

    def greet(k, carry):
        pl.semaphore_signal(barrier, inc=1, device_id=y_peer(k), device_id_type=MESH)
        pl.semaphore_signal(barrier, inc=1, device_id=z_peer(k), device_id_type=MESH)
        return carry

    lax.fori_loop(1, N, greet, 0)
    for peer in (xh_peer, sib_peer, lo_peer, far_peer):
        pl.semaphore_signal(barrier, inc=1, device_id=peer, device_id_type=MESH)

    def y_rows(k):
        return pl.ds(pl.multiple_of(16 * lax.rem(t + k, N), 16), 16)

    my_rows = y_rows(0)
    mine = 16 + c * 8 + z
    other = c * 8 + z

    load_cot.wait()
    cot_own = jnp.concatenate([cot_ref[0].astype(F32), cot_ref[1].astype(F32)], axis=0)
    cg[mine] = cot_own.astype(BF16)

    row = lax.broadcasted_iota(jnp.int32, (256, 256), 0)
    col = lax.broadcasted_iota(jnp.int32, (256, 256), 1)
    x_half = jnp.where(row // 128 == 1, xh, 1 - xh)
    owner = x_half * 16 + (lax.rem(row, 64) // 8) * 2 + lax.rem(row, 128) // 64
    token = (lax.rem(row, 8) // 4) * 128 + owner * 4 + lax.rem(row, 4)
    perm = jnp.where(col == token, 1.0, 0.0).astype(BF16)
    load_x.wait()
    x_flat = x_in[...].reshape(256, FEAT)
    xs = jnp.dot(perm, x_flat, preferred_element_type=F32)
    xp[...] = xs
    load_gain.wait()
    gain = gain_ref[...]
    u[...] = (xs * gain).astype(BF16).reshape(2, 128, FEAT)
    load_w1.wait()
    s_a[...] = (
        jnp.dot(u[...].reshape(256, FEAT), w1[...], preferred_element_type=F32)
        .astype(BF16)
        .reshape(2, 128, HID)
    )
    pl.semaphore_wait(barrier, 2 * (N - 1) + 4)
    a_y = Phase(lambda k: (s_a.at[:, y_rows(k)], r_a.at[k], y_peer(k)), 1, N, sems, r_a.at[pl.ds(1, N - 1)])
    a_y.start()
    to_xh = Phase(lambda k: (cg.at[mine], cg.at[other], xh_peer), 0, 1, sems)
    to_xh.start()
    to_z = Phase(lambda k: (cg.at[mine], cg.at[mine], z_peer(k)), 1, N, sems, cg.at[pl.ds(0, N - 1)])
    to_z.start()

    ones = jnp.ones((8, FEAT), BF16)
    squares = []
    for h in range(2):
        rows = xp[h * 128 : (h + 1) * 128, :]
        sq = rows * rows
        hi = sq.astype(BF16)
        lo = (sq - hi.astype(F32)).astype(BF16)
        squares.append(
            lax.dot_general(ones, hi, NT, preferred_element_type=F32)
            + lax.dot_general(ones, lo, NT, preferred_element_type=F32)
        )
    place = lax.broadcasted_iota(jnp.int32, (8, 128), 0)
    s_sq[...] = jnp.where(place == 0, squares[0], squares[1])
    sq_y = Phase(lambda k: (s_sq, r_sq.at[k], y_peer(k)), 1, N, sems, r_sq.at[pl.ds(1, N - 1)])
    sq_y.start()

    to_xh.arrived()
    to_z2 = Phase(lambda k: (cg.at[other], cg.at[other], z_peer(k)), 1, N, sems, cg.at[pl.ds(0, N - 1)])
    to_z2.start()
    core_rows = pl.ds(pl.multiple_of(64 * c, 64), 64)
    u_lo = Phase(lambda k: (u.at[:, core_rows], u_o.at[:, core_rows], lo_peer), 0, 1, sems)
    u_lo.start()

    def pieces(h):
        return pl.ds(h * 16 + c * 8, 8)

    def gathered(h):
        return Phase(lambda k: (cg.at[pieces(h)], cg.at[pieces(h)], sib_peer), 0, 1, sems)

    def crossed(h):
        return Phase(lambda k: (cg.at[pieces(h)], cg_o.at[pieces(h)], lo_peer), 0, 1, sems)

    def rows_of(pieces_ref, h):
        return pieces_ref[h * 16 : (h + 1) * 16].astype(F32).reshape(128, FEAT).astype(BF16)

    c_y = [
        Phase(
            lambda k, h=h: (s_c.at[h, y_rows(k)], r_c.at[h, k], y_peer(k)),
            1,
            N,
            sems,
            r_c.at[h, pl.ds(1, N - 1)],
        )
        for h in range(2)
    ]

    def send_c(h):
        s_c[h] = lax.dot_general(
            rows_of(cg, h), w2[...], NT, preferred_element_type=F32
        ).astype(BF16)
        c_y[h].start()

    load_w2.wait()
    to_z.arrived()
    cot_sib1 = gathered(1)
    cot_sib1.start()
    cot_sib1.arrived()
    send_c(1)
    cot_lo1 = crossed(1)
    cot_lo1.start()

    sq_y.arrived()
    total_sq = s_sq[...]
    for k in range(1, N):
        total_sq = total_sq + r_sq[k]
    lane = lax.broadcasted_iota(jnp.int32, (16, 128), 1)
    spot = lax.broadcasted_iota(jnp.int32, (16, 128), 0) + 16 * t
    a_y.arrived()
    for h in range(2):
        picked = jnp.where(lane == spot, jnp.broadcast_to(total_sq[h : h + 1, :], (16, 128)), 0.0)
        scale = lax.rsqrt(jnp.sum(picked, axis=1, keepdims=True) / D + EPSILON)
        sums = s_a[h, my_rows].astype(F32)
        for k in range(1, N):
            sums = sums + r_a[k, h].astype(F32)
        pre = sums * scale
        sig = jax.nn.sigmoid(pre)
        hid[h, my_rows] = (pre * sig).astype(BF16)
        p_own[h] = sums
        slope[h] = sig * (1.0 + pre * (1.0 - sig))
        scl[h] = jnp.broadcast_to(scale, (16, 128))

    b_near = Phase(
        lambda k: (hid.at[:, my_rows], hid.at[:, my_rows], y_peer(1 + 6 * k)),
        0,
        2,
        sems,
        hid.at[:, pl.ds(0, 32)],
    )
    b_near.start()

    to_z2.arrived()
    cot_sib0 = gathered(0)
    cot_sib0.start()
    cot_sib0.arrived()
    send_c(0)
    cot_lo0 = crossed(0)
    cot_lo0.start()

    b_near.arrived()

    def pass_on(k):
        side, step = k // 2, k % 2 + 1
        rows = y_rows(1 if side else N - 1)
        return hid.at[:, rows], hid.at[:, rows], y_peer(N - step if side else step)

    def pass_far(k):
        rows = y_rows(1 if k else N - 1)
        return hid.at[k, rows], hid.at[k, rows], y_peer(N - 3 if k else 3)

    b_rest = (
        Phase(pass_far, 0, 2, sems, hid.at[0, pl.ds(0, 32)]),
        Phase(pass_on, 0, 4, sems, hid.at[:, pl.ds(0, 64)]),
    )
    for phase in b_rest:
        phase.start()

    d_y = [
        Phase(
            lambda k, h=h: (q.at[h, my_rows], q.at[h, my_rows], y_peer(k)),
            1,
            N,
            sems,
            q.at[h, pl.ds(0, 16 * (N - 1))],
        )
        for h in range(2)
    ]
    for h in (1, 0):
        c_y[h].arrived()
        sums = s_c[h, my_rows].astype(F32)
        for k in range(1, N):
            sums = sums + r_c[h, k].astype(F32)
        scale = scl[h][:, :1]
        own = sums * slope[h] * scale
        q[h, my_rows] = own.astype(BF16)
        if h == 0:
            d_y[0].start()
        inner = jnp.sum(own * p_own[h], axis=1, keepdims=True) * (scale * scale / D)
        e_s[:, h * 128 : (h + 1) * 128] = jnp.sum(
            jnp.where(lane == spot, inner, 0.0), axis=0, keepdims=True
        )
    e_y = Phase(lambda k: (e_s, e_r.at[k], y_peer(k)), 1, N, sems, e_r.at[pl.ds(1, N - 1)])
    e_y.start()
    d_y[1].start()

    for phase in b_rest:
        phase.arrived()
    hid_lo = Phase(lambda k: (hid, hid_o, lo_peer), 0, 1, sems)
    hid_lo.start()
    branch[...] = jnp.dot(
        hid[...].reshape(256, HID), w2[...], preferred_element_type=F32
    ).reshape(2, 128, FEAT)
    sib_rows = pl.ds(pl.multiple_of(64 - 64 * c, 64), 64)
    f_sib = Phase(lambda k: (branch.at[:, sib_rows], r_fs, sib_peer), 0, 1, sems)
    f_sib.start()

    u_lo.arrived()
    u_sib = Phase(lambda k: (u_o.at[:, core_rows], u_o.at[:, core_rows], sib_peer), 0, 1, sems)
    u_sib.start()

    f_sib.arrived()
    for h in range(2):
        both = branch[h, core_rows] + r_fs[h]
        s_fz[h] = both.reshape(N, 8, FEAT).astype(BF16)

    def f_near(k):
        step = N - 1 if k % 2 else 1
        if k < 2:
            return s_fz.at[:, z_place(2 * step)], r_fz.at[k], z_peer(step)
        return s_fz.at[k - 2, z_place(4)], r_ff.at[k - 2], z_peer(step)

    f_one = Phase(f_near, 0, 2, sems, r_fz)
    f_one.start()
    f_four = Phase(lambda k: f_near(k + 2), 0, 2, sems, r_ff)
    f_four.start()

    g_sibs = [
        Phase(lambda k, h=h: (big.at[h, sib_rows], r_gs.at[h], sib_peer), 0, 1, sems)
        for h in range(2)
    ]
    g_zs = [
        Phase(
            lambda k, h=h: (s_gz.at[h, z_place(k)], r_gz.at[h, k], z_peer(k)),
            1,
            N,
            sems,
            r_gz.at[h, pl.ds(1, N - 1)],
        )
        for h in range(2)
    ]
    q_lo = [
        Phase(lambda k, h=h: (q.at[h], q_o.at[h], lo_peer), 0, 1, sems)
        for h in range(2)
    ]
    f_far = Phase(
        lambda k: (s_fz.at[:, z_place(FAR[k])], r_f2.at[k], z_peer(FAR[k])), 0, 4, sems, r_f2
    )

    def pass_f():
        f_one.arrived()
        f_four.arrived()
        for k, step in ((0, 1), (1, N - 1)):
            to = z_place(step)
            for h in range(2):
                s_fz[h, to] = (s_fz[h, to].astype(F32) + r_fz[k, h].astype(F32)).astype(BF16)
            to = z_place(3 * step)
            s_fz[k, to] = (s_fz[k, to].astype(F32) + r_ff[k].astype(F32)).astype(BF16)
        f_far.start()

    ee_sib = Phase(lambda k: (ee_own, ee_r1, sib_peer), 0, 1, sems)
    ee_z = Phase(lambda k: (ee_chip, ee_rz.at[k], z_peer(k)), 1, N, sems, ee_rz.at[pl.ds(1, N - 1)])
    gain_part = jnp.zeros((1, FEAT), F32)
    for h in range(2):
        d_y[h].arrived()
        for rows in (sib_rows, core_rows):
            part = lax.dot_general(q[h, rows], w1[...], NT, preferred_element_type=F32)
            big[h, rows] = part
            if rows is sib_rows:
                g_sibs[h].start()
        if h == 0:
            e_y.arrived()
            e_sum = e_s[...]
            for k in range(1, N):
                e_sum = e_sum + e_r[k]
            ee_own[...] = e_sum
            ee_sib.start()
        q_lo[h].start()
        gain_part = gain_part + jnp.sum(
            big[h] * xp[h * 128 : (h + 1) * 128, :], axis=0, keepdims=True
        )
        if h == 0:
            pass_f()
        else:
            gg_own[...] = gain_part
            gg_sib = Phase(lambda k: (gg_own, gg_r1, sib_peer), 0, 1, sems)
            gg_sib.start()
        g_sibs[h].arrived()
        both = big[h, core_rows] + r_gs[h]
        s_gz[h] = both.reshape(N, 8, FEAT).astype(BF16)
        if h == 1:
            gg_sib.arrived()
            gg_chip[...] = gg_own[...] + gg_r1[...]
            gg_z = Phase(
                lambda k: (gg_chip, gg_rz.at[k], z_peer(k)), 1, N, sems, gg_rz.at[pl.ds(1, N - 1)]
            )
            gg_z.start()
        g_zs[h].start()
        if h == 0:
            ee_sib.arrived()
            ee_chip[...] = ee_own[...] + ee_r1[...]
            ee_z.start()

    cot_sibo = [
        Phase(lambda k, h=h: (cg_o.at[pieces(h)], cg_o.at[pieces(h)], sib_peer), 0, 1, sems)
        for h in range(2)
    ]
    cot_lo1.arrived()
    cot_sibo[1].start()
    cot_lo0.arrived()
    cot_sibo[0].start()
    hid_lo.arrived()
    for h in range(2):
        cot_sibo[h].arrived()
    hid_all = jnp.concatenate(
        [hid[...].reshape(256, HID), hid_o[...].reshape(256, HID)], axis=0
    )
    cot_all = jnp.concatenate(
        [rows_of(cg, 0), rows_of(cg, 1), rows_of(cg_o, 0), rows_of(cg_o, 1)], axis=0
    )
    second_out[...] = lax.dot_general(
        hid_all, cot_all, TN, preferred_element_type=F32
    ).astype(BF16)

    def z_total(sent, received, h):
        total = sent[h, z].astype(F32)
        for k in range(1, N):
            total = total + received(k)
        return total

    def f_total(h):
        total = s_fz[h, z].astype(F32)
        for k in range(4):
            total = total + r_f2[k, h].astype(F32)
        return total

    ee_z.arrived()
    ee_total = ee_chip[...]
    for k in range(1, N):
        ee_total = ee_total + ee_rz[k]
    ee_line[...] = ee_total
    ee_xh = Phase(lambda k: (ee_line, ee_rx, xh_peer), 0, 1, sems)
    ee_xh.start()

    f_far.arrived()
    s_fx[...] = f_total(0)
    f_xh = Phase(lambda k: (s_fx, r_fx, xh_peer), 0, 1, sems)
    f_xh.start()
    own_branch = f_total(1)

    g_zs[0].arrived()
    s_gx[...] = z_total(s_gz, lambda k: r_gz[0, k].astype(F32), 0)
    g_xh = Phase(lambda k: (s_gx, r_gx, xh_peer), 0, 1, sems)
    g_xh.start()

    gg_z.arrived()
    gg_total = gg_chip[...]
    for k in range(1, N):
        gg_total = gg_total + gg_rz[k]
    gg_line[...] = gg_total
    x_peers = (xh_peer, lo_peer, far_peer)
    gg_x = Phase(lambda k: (gg_line, gg_rx.at[k], x_peers[k]), 0, 3, sems, gg_rx)
    gg_x.start()

    u_sib.arrived()
    for h in range(2):
        q_lo[h].arrived()
    u_all = jnp.concatenate([u[...].reshape(256, FEAT), u_o[...].reshape(256, FEAT)], axis=0)
    q_all = jnp.concatenate(
        [q[...].reshape(256, HID), q_o[...].reshape(256, HID)], axis=0
    )
    first_out[...] = lax.dot_general(u_all, q_all, TN, preferred_element_type=F32).astype(BF16)

    x_own = xp[pl.ds(pl.multiple_of(mine * 8, 8), 8), :]
    f_xh.arrived()
    outputs = x_own + own_branch + r_fx[...]
    out_ref[0] = outputs[0:4].astype(BF16)
    out_ref[1] = outputs[4:8].astype(BF16)

    g_zs[1].arrived()
    normed_grad = z_total(s_gz, lambda k: r_gz[1, k].astype(F32), 1)
    g_xh.arrived()
    normed_grad = normed_grad + r_gx[...]
    ee_xh.arrived()
    inner_row = ee_line[:, 128:256] + ee_rx[:, 0:128]
    own_lane = lax.broadcasted_iota(jnp.int32, (8, 128), 1)
    own_spot = lax.broadcasted_iota(jnp.int32, (8, 128), 0) + c * 64 + z * 8
    inner = jnp.sum(
        jnp.where(own_lane == own_spot, jnp.broadcast_to(inner_row, (8, 128)), 0.0),
        axis=1,
        keepdims=True,
    )
    grads = cg[mine].astype(F32) + gain * normed_grad - x_own * inner
    ing_ref[0] = grads[0:4].astype(BF16)
    ing_ref[1] = grads[4:8].astype(BF16)
    gg_x.arrived()
    gg_ref[...] = (gg_line[...] + gg_rx[0]) + (gg_rx[1] + gg_rx[2])

    for phase in sems["phases"][-SENDS:]:
        phase.sent()


def save(*refs):
    sources, targets, sems = refs[:5], refs[5:10], refs[10]
    copies = [pltpu.make_async_copy(sources[i], targets[i], sems.at[i]) for i in range(5)]
    for copy in copies:
        copy.start()
    for copy in copies:
        copy.wait()


def per_device(inputs, gain, w_first, w_second, cotangent):
    vmem = pl.BlockSpec(memory_space=pltpu.VMEM)
    hbm = pl.BlockSpec(memory_space=pltpu.HBM)
    anywhere = pl.BlockSpec(memory_space=pl.ANY)
    shapes = [
        ((2, 128, FEAT), BF16),
        ((1, FEAT), F32),
        ((FEAT, HID), BF16),
        ((HID, FEAT), BF16),
        ((2, 4, FEAT), BF16),
        ((256, FEAT), F32),
        ((2, 128, FEAT), BF16),
        ((2, 128, FEAT), BF16),
        ((32, 8, FEAT), BF16),
        ((32, 8, FEAT), BF16),
        ((2, 128, HID), BF16),
        ((N, 2, 16, HID), BF16),
        ((8, 128), F32),
        ((N, 8, 128), F32),
        ((2, 128, HID), BF16),
        ((2, N, 16, HID), BF16),
        ((2, 128, HID), BF16),
        ((2, 128, HID), BF16),
        ((2, 128, HID), BF16),
        ((2, 128, HID), BF16),
        ((2, 16, HID), F32),
        ((2, 16, HID), F32),
        ((2, 16, 128), F32),
        ((2, 128, FEAT), F32),
        ((2, 64, FEAT), F32),
        ((2, N, 8, FEAT), BF16),
        ((2, 2, 8, FEAT), BF16),
        ((2, 8, FEAT), BF16),
        ((4, 2, 8, FEAT), BF16),
        ((8, FEAT), F32),
        ((8, FEAT), F32),
        ((2, 128, FEAT), F32),
        ((2, 64, FEAT), F32),
        ((2, N, 8, FEAT), BF16),
        ((2, N, 8, FEAT), BF16),
        ((8, FEAT), F32),
        ((8, FEAT), F32),
        ((1, 256), F32),
        ((N, 1, 256), F32),
        ((1, 256), F32),
        ((1, 256), F32),
        ((1, 256), F32),
        ((N, 1, 256), F32),
        ((1, 256), F32),
        ((1, 256), F32),
        ((1, FEAT), F32),
        ((1, FEAT), F32),
        ((1, FEAT), F32),
        ((N, 1, FEAT), F32),
        ((1, FEAT), F32),
        ((3, 1, FEAT), F32),
    ]
    results = (
        jax.ShapeDtypeStruct(cotangent.shape, BF16),
        jax.ShapeDtypeStruct(cotangent.shape, BF16),
        jax.ShapeDtypeStruct(w_first.shape, BF16),
        jax.ShapeDtypeStruct(w_second.shape, BF16),
        jax.ShapeDtypeStruct((1, FEAT), F32),
    )
    made = pl.pallas_call(
        kernel,
        out_shape=results,
        in_specs=[hbm] * 5,
        out_specs=(vmem,) * 5,
        scratch_shapes=[pltpu.VMEM(shape, dtype) for shape, dtype in shapes]
        + [
            pltpu.SemaphoreType.DMA((SENDS,)),
            pltpu.SemaphoreType.DMA((PHASES,)),
            pltpu.SemaphoreType.DMA((5,)),
        ],
        compiler_params=pltpu.CompilerParams(
            collective_id=0, has_side_effects=True, vmem_limit_bytes=48 * 1024 * 1024
        ),
    )(
        *(
            pltpu.with_memory_space_constraint(array, pltpu.HBM)
            for array in (inputs, gain.reshape(1, FEAT), w_first, w_second, cotangent)
        )
    )
    outputs, input_grad, first_grad, second_grad, gain_grad = pl.pallas_call(
        save,
        out_shape=results,
        in_specs=[vmem] * 5,
        out_specs=(anywhere,) * 5,
        scratch_shapes=[pltpu.SemaphoreType.DMA((5,))],
        compiler_params=pltpu.CompilerParams(vmem_limit_bytes=4 * 1024 * 1024),
    )(*(pltpu.with_memory_space_constraint(array, pltpu.VMEM) for array in made))
    return outputs, input_grad, first_grad, second_grad, gain_grad.reshape(FEAT)


def solution(mesh):
    in_specs = (
        P(None, "section", "tensor"),
        P("tensor"),
        P("tensor", "dp"),
        P("dp", "tensor"),
        P(None, ("section", "dp"), "tensor"),
    )
    out_specs = (
        P(None, ("section", "dp"), "tensor"),
        P(None, ("section", "dp"), "tensor"),
        P("tensor", "dp"),
        P("dp", "tensor"),
        P("tensor"),
    )
    return jax.shard_map(
        per_device, mesh=mesh, in_specs=in_specs, out_specs=out_specs, check_vma=False
    )
```

```python
import jax
import jax.numpy as jnp
from jax import lax
from jax.experimental import pallas as pl
from jax.experimental.pallas import tpu as pltpu
from jax.sharding import PartitionSpec as P

MESH = pl.DeviceIdType.MESH
F32 = jnp.float32
BF16 = jnp.bfloat16
D = 8192
EPSILON = 1e-06
N = 8
HID = 512
FEAT = 1024
NT = (((1,), (1,)), ((), ()))
TN = (((0,), (0,)), ((), ()))


class Phase:
    def __init__(self, make, first, last, sems, whole=None):
        self.make, self.first, self.last, self.sems, self.whole = make, first, last, sems, whole
        self.place = sems["used"]
        sems["used"] += 1

    def describe(self, src, dst, device):
        return pltpu.make_async_remote_copy(
            src_ref=src,
            dst_ref=dst,
            send_sem=self.sems["send"].at[self.send_place],
            recv_sem=self.sems["recv"].at[self.place],
            device_id=device,
            device_id_type=MESH,
        )

    def start(self):
        phases = self.sems["phases"]
        self.send_place = len(phases) % SENDS
        if len(phases) >= SENDS:
            phases[-SENDS].sent()
        phases.append(self)
        order = FARTHEST_FIRST if self.last == N else range(self.first, self.last)
        for k in order:
            self.describe(*self.make(k)).start()

    def all(self):
        src, dst, device = self.make(self.first)
        if self.whole is not None:
            src = dst = self.whole
        return self.describe(src, dst, device)

    def arrived(self):
        self.all().wait_recv()

    def sent(self):
        self.all().wait_send()


SENDS = 16
FARTHEST_FIRST = (3, 5, 4, 2, 6, 1, 7)
PHASES = 38


def kernel(
    x_hbm, gain_hbm, w1_hbm, w2_hbm, cot_hbm,
    out_ref, ing_ref, first_out, second_out, gg_ref,
    x_in, gain_ref, w1, w2, cot_ref, xp, u, u_o, cg, cg_o,
    s_a, r_a, s_sq, r_sq, s_c, r_c, hid, hid_o, q, q_o, p_own, slope, scl,
    branch, r_fs, s_fz, r_fz, s_fx, r_fx,
    big, r_gs, s_gz, r_gz, s_gx, r_gx,
    e_s, e_r, ee_own, ee_r1, ee_chip, ee_rz, ee_line, ee_rx, gg_own, gg_r1, gg_chip, gg_rz, gg_line, gg_rx,
    send_sems, recv_sems, local_sems,
):
    s = lax.axis_index("section")
    d = lax.axis_index("dp")
    t = lax.axis_index("tensor")
    xh = d // 16
    z = lax.rem(d // 2, N)
    c = lax.rem(d, 2)

    def y_peer(k):
        return {"section": s, "dp": d, "tensor": lax.rem(t + k, N)}

    def z_place(k):
        return lax.rem(z + k, N)

    def z_peer(k):
        return {"section": s, "dp": xh * 16 + z_place(k) * 2 + c, "tensor": t}

    xh_peer = {"section": s, "dp": lax.rem(d + 16, 32), "tensor": t}
    sib_peer = {"section": s, "dp": d + 1 - 2 * c, "tensor": t}
    lo_peer = {"section": 1 - s, "dp": d, "tensor": t}
    far_peer = {"section": 1 - s, "dp": lax.rem(d + 16, 32), "tensor": t}

    sems = {"used": 0, "send": send_sems, "recv": recv_sems, "phases": []}

    load_cot = pltpu.make_async_copy(cot_hbm, cot_ref, local_sems.at[0])
    load_gain = pltpu.make_async_copy(gain_hbm, gain_ref, local_sems.at[1])
    load_x = pltpu.make_async_copy(x_hbm, x_in, local_sems.at[2])
    load_w1 = pltpu.make_async_copy(w1_hbm, w1, local_sems.at[3])
    load_w2 = pltpu.make_async_copy(w2_hbm, w2, local_sems.at[4])
    for load in (load_cot, load_gain, load_x, load_w1, load_w2):
        load.start()

    barrier = pltpu.get_barrier_semaphore()

    def greet(k, carry):
        pl.semaphore_signal(barrier, inc=1, device_id=y_peer(k), device_id_type=MESH)
        pl.semaphore_signal(barrier, inc=1, device_id=z_peer(k), device_id_type=MESH)
        return carry

    lax.fori_loop(1, N, greet, 0)
    for peer in (xh_peer, sib_peer, lo_peer, far_peer):
        pl.semaphore_signal(barrier, inc=1, device_id=peer, device_id_type=MESH)

    def y_rows(k):
        return pl.ds(pl.multiple_of(16 * lax.rem(t + k, N), 16), 16)

    my_rows = y_rows(0)
    mine = 16 + c * 8 + z
    other = c * 8 + z

    load_cot.wait()
    cot_own = jnp.concatenate([cot_ref[0].astype(F32), cot_ref[1].astype(F32)], axis=0)
    cg[mine] = cot_own.astype(BF16)

    row = lax.broadcasted_iota(jnp.int32, (256, 256), 0)
    col = lax.broadcasted_iota(jnp.int32, (256, 256), 1)
    x_half = jnp.where(row // 128 == 1, xh, 1 - xh)
    owner = x_half * 16 + (lax.rem(row, 64) // 8) * 2 + lax.rem(row, 128) // 64
    token = (lax.rem(row, 8) // 4) * 128 + owner * 4 + lax.rem(row, 4)
    perm = jnp.where(col == token, 1.0, 0.0).astype(BF16)
    load_x.wait()
    x_flat = x_in[...].reshape(256, FEAT)
    xs = jnp.dot(perm, x_flat, preferred_element_type=F32)
    xp[...] = xs
    load_gain.wait()
    gain = gain_ref[...]
    u[...] = (xs * gain).astype(BF16).reshape(2, 128, FEAT)
    load_w1.wait()
    s_a[...] = (
        jnp.dot(u[...].reshape(256, FEAT), w1[...], preferred_element_type=F32)
        .astype(BF16)
        .reshape(2, 128, HID)
    )
    pl.semaphore_wait(barrier, 2 * (N - 1) + 4)
    a_y = Phase(lambda k: (s_a.at[:, y_rows(k)], r_a.at[k], y_peer(k)), 1, N, sems, r_a.at[pl.ds(1, N - 1)])
    a_y.start()
    to_xh = Phase(lambda k: (cg.at[mine], cg.at[other], xh_peer), 0, 1, sems)
    to_xh.start()
    to_z = Phase(lambda k: (cg.at[mine], cg.at[mine], z_peer(k)), 1, N, sems, cg.at[pl.ds(0, N - 1)])
    to_z.start()

    ones = jnp.ones((8, FEAT), BF16)
    squares = []
    for h in range(2):
        rows = xp[h * 128 : (h + 1) * 128, :]
        sq = rows * rows
        hi = sq.astype(BF16)
        lo = (sq - hi.astype(F32)).astype(BF16)
        squares.append(
            lax.dot_general(ones, hi, NT, preferred_element_type=F32)
            + lax.dot_general(ones, lo, NT, preferred_element_type=F32)
        )
    place = lax.broadcasted_iota(jnp.int32, (8, 128), 0)
    s_sq[...] = jnp.where(place == 0, squares[0], squares[1])
    sq_y = Phase(lambda k: (s_sq, r_sq.at[k], y_peer(k)), 1, N, sems, r_sq.at[pl.ds(1, N - 1)])
    sq_y.start()

    to_xh.arrived()
    to_z2 = Phase(lambda k: (cg.at[other], cg.at[other], z_peer(k)), 1, N, sems, cg.at[pl.ds(0, N - 1)])
    to_z2.start()
    core_rows = pl.ds(pl.multiple_of(64 * c, 64), 64)
    u_lo = Phase(lambda k: (u.at[:, core_rows], u_o.at[:, core_rows], lo_peer), 0, 1, sems)
    u_lo.start()

    def pieces(h):
        return pl.ds(h * 16 + c * 8, 8)

    def gathered(h):
        return Phase(lambda k: (cg.at[pieces(h)], cg.at[pieces(h)], sib_peer), 0, 1, sems)

    def crossed(h):
        return Phase(lambda k: (cg.at[pieces(h)], cg_o.at[pieces(h)], lo_peer), 0, 1, sems)

    def rows_of(pieces_ref, h):
        return pieces_ref[h * 16 : (h + 1) * 16].astype(F32).reshape(128, FEAT).astype(BF16)

    c_y = [
        Phase(
            lambda k, h=h: (s_c.at[h, y_rows(k)], r_c.at[h, k], y_peer(k)),
            1,
            N,
            sems,
            r_c.at[h, pl.ds(1, N - 1)],
        )
        for h in range(2)
    ]

    def send_c(h):
        s_c[h] = lax.dot_general(
            rows_of(cg, h), w2[...], NT, preferred_element_type=F32
        ).astype(BF16)
        c_y[h].start()

    load_w2.wait()
    to_z.arrived()
    cot_sib1 = gathered(1)
    cot_sib1.start()
    cot_sib1.arrived()
    send_c(1)
    cot_lo1 = crossed(1)
    cot_lo1.start()

    sq_y.arrived()
    total_sq = s_sq[...]
    for k in range(1, N):
        total_sq = total_sq + r_sq[k]
    lane = lax.broadcasted_iota(jnp.int32, (16, 128), 1)
    spot = lax.broadcasted_iota(jnp.int32, (16, 128), 0) + 16 * t
    a_y.arrived()
    for h in range(2):
        picked = jnp.where(lane == spot, jnp.broadcast_to(total_sq[h : h + 1, :], (16, 128)), 0.0)
        scale = lax.rsqrt(jnp.sum(picked, axis=1, keepdims=True) / D + EPSILON)
        sums = s_a[h, my_rows].astype(F32)
        for k in range(1, N):
            sums = sums + r_a[k, h].astype(F32)
        pre = sums * scale
        sig = jax.nn.sigmoid(pre)
        hid[h, my_rows] = (pre * sig).astype(BF16)
        p_own[h] = sums
        slope[h] = sig * (1.0 + pre * (1.0 - sig))
        scl[h] = jnp.broadcast_to(scale, (16, 128))

    b_near = Phase(
        lambda k: (hid.at[:, my_rows], hid.at[:, my_rows], y_peer(1 + 6 * k)),
        0,
        2,
        sems,
        hid.at[:, pl.ds(0, 32)],
    )
    b_near.start()

    to_z2.arrived()
    cot_sib0 = gathered(0)
    cot_sib0.start()
    cot_sib0.arrived()
    send_c(0)
    cot_lo0 = crossed(0)
    cot_lo0.start()

    b_near.arrived()

    def pass_on(k):
        side, step = k // 2, k % 2 + 1
        rows = y_rows(1 if side else N - 1)
        return hid.at[:, rows], hid.at[:, rows], y_peer(N - step if side else step)

    def pass_far(k):
        rows = y_rows(1 if k else N - 1)
        return hid.at[k, rows], hid.at[k, rows], y_peer(N - 3 if k else 3)

    b_rest = (
        Phase(pass_far, 0, 2, sems, hid.at[0, pl.ds(0, 32)]),
        Phase(pass_on, 0, 4, sems, hid.at[:, pl.ds(0, 64)]),
    )
    for phase in b_rest:
        phase.start()

    d_y = [
        Phase(
            lambda k, h=h: (q.at[h, my_rows], q.at[h, my_rows], y_peer(k)),
            1,
            N,
            sems,
            q.at[h, pl.ds(0, 16 * (N - 1))],
        )
        for h in range(2)
    ]
    for h in (1, 0):
        c_y[h].arrived()
        sums = s_c[h, my_rows].astype(F32)
        for k in range(1, N):
            sums = sums + r_c[h, k].astype(F32)
        scale = scl[h][:, :1]
        own = sums * slope[h] * scale
        q[h, my_rows] = own.astype(BF16)
        if h == 0:
            d_y[0].start()
        inner = jnp.sum(own * p_own[h], axis=1, keepdims=True) * (scale * scale / D)
        e_s[:, h * 128 : (h + 1) * 128] = jnp.sum(
            jnp.where(lane == spot, inner, 0.0), axis=0, keepdims=True
        )
    e_y = Phase(lambda k: (e_s, e_r.at[k], y_peer(k)), 1, N, sems, e_r.at[pl.ds(1, N - 1)])
    e_y.start()
    d_y[1].start()

    for phase in b_rest:
        phase.arrived()
    sib_rows = pl.ds(pl.multiple_of(64 - 64 * c, 64), 64)
    f_sibs = [
        Phase(lambda k, h=h: (branch.at[h, sib_rows], r_fs.at[h], sib_peer), 0, 1, sems)
        for h in range(2)
    ]
    for h in range(2):
        branch[h] = jnp.dot(hid[h], w2[...], preferred_element_type=F32)
        f_sibs[h].start()

    u_lo.arrived()
    u_sib = Phase(lambda k: (u_o.at[:, core_rows], u_o.at[:, core_rows], sib_peer), 0, 1, sems)
    u_sib.start()

    f_sibs[0].arrived()
    s_fx[...] = (branch[0, core_rows] + r_fs[0]).astype(BF16)
    f_xh = Phase(lambda k: (s_fx, r_fx, xh_peer), 0, 1, sems)
    f_xh.start()
    hid_lo = Phase(lambda k: (hid, hid_o, lo_peer), 0, 1, sems)
    hid_lo.start()
    f_z = Phase(
        lambda k: (s_fz.at[z_place(k)], r_fz.at[k], z_peer(k)), 1, N, sems, r_fz.at[pl.ds(1, N - 1)]
    )
    cot_sibo = [
        Phase(lambda k, h=h: (cg_o.at[pieces(h)], cg_o.at[pieces(h)], sib_peer), 0, 1, sems)
        for h in range(2)
    ]
    cot_lo1.arrived()
    cot_sibo[1].start()
    cot_lo0.arrived()
    cot_sibo[0].start()

    g_sibs = [
        Phase(lambda k, h=h: (big.at[h, sib_rows], r_gs.at[h], sib_peer), 0, 1, sems)
        for h in range(2)
    ]
    g_xh = Phase(lambda k: (s_gx, r_gx, xh_peer), 0, 1, sems)
    g_z = Phase(
        lambda k: (s_gz.at[z_place(k)], r_gz.at[k], z_peer(k)), 1, N, sems, r_gz.at[pl.ds(1, N - 1)]
    )
    q_lo = [
        Phase(lambda k, h=h: (q.at[h], q_o.at[h], lo_peer), 0, 1, sems)
        for h in range(2)
    ]
    ee_sib = Phase(lambda k: (ee_own, ee_r1, sib_peer), 0, 1, sems)
    ee_z = Phase(lambda k: (ee_chip, ee_rz.at[k], z_peer(k)), 1, N, sems, ee_rz.at[pl.ds(1, N - 1)])

    def normed_part(h):
        d_y[h].arrived()
        for rows in (sib_rows, core_rows):
            big[h, rows] = lax.dot_general(
                q[h, rows], w1[...], NT, preferred_element_type=F32
            )
            if rows is sib_rows:
                g_sibs[h].start()

    def gain_part(h):
        return jnp.sum(big[h] * xp[h * 128 : (h + 1) * 128, :], axis=0, keepdims=True)

    normed_part(0)
    e_y.arrived()
    e_sum = e_s[...]
    for k in range(1, N):
        e_sum = e_sum + e_r[k]
    ee_own[...] = e_sum
    ee_sib.start()
    g_sibs[0].arrived()
    s_gx[...] = (big[0, core_rows] + r_gs[0]).astype(BF16)
    g_xh.start()
    ee_sib.arrived()
    ee_chip[...] = ee_own[...] + ee_r1[...]
    ee_z.start()
    q_lo[0].start()
    gain_first = gain_part(0)

    normed_part(1)
    gg_own[...] = gain_first + gain_part(1)
    gg_sib = Phase(lambda k: (gg_own, gg_r1, sib_peer), 0, 1, sems)
    gg_sib.start()
    f_sibs[1].arrived()
    f_xh.arrived()
    f_sum = branch[1, core_rows] + r_fs[1] + r_fx[...].astype(F32)
    s_fz[...] = f_sum.reshape(N, 8, FEAT).astype(BF16)
    f_z.start()
    gg_sib.arrived()
    gg_chip[...] = gg_own[...] + gg_r1[...]
    gg_z = Phase(lambda k: (gg_chip, gg_rz.at[k], z_peer(k)), 1, N, sems, gg_rz.at[pl.ds(1, N - 1)])
    gg_z.start()
    g_sibs[1].arrived()
    g_xh.arrived()
    g_sum = big[1, core_rows] + r_gs[1] + r_gx[...].astype(F32)
    s_gz[...] = g_sum.reshape(N, 8, FEAT).astype(BF16)
    g_z.start()
    q_lo[1].start()

    hid_lo.arrived()
    for h in range(2):
        cot_sibo[h].arrived()
    hid_all = jnp.concatenate(
        [hid[...].reshape(256, HID), hid_o[...].reshape(256, HID)], axis=0
    )
    cot_all = jnp.concatenate(
        [rows_of(cg, 0), rows_of(cg, 1), rows_of(cg_o, 0), rows_of(cg_o, 1)], axis=0
    )
    second_out[...] = lax.dot_general(
        hid_all, cot_all, TN, preferred_element_type=F32
    ).astype(BF16)

    def z_total(sent, received):
        total = sent[z].astype(F32)
        for k in range(1, N):
            total = total + received[k].astype(F32)
        return total

    ee_z.arrived()
    ee_total = ee_chip[...]
    for k in range(1, N):
        ee_total = ee_total + ee_rz[k]
    ee_line[...] = ee_total
    ee_xh = Phase(lambda k: (ee_line, ee_rx, xh_peer), 0, 1, sems)
    ee_xh.start()

    gg_z.arrived()
    gg_total = gg_chip[...]
    for k in range(1, N):
        gg_total = gg_total + gg_rz[k]
    gg_line[...] = gg_total
    x_peers = (xh_peer, lo_peer, far_peer)
    gg_x = Phase(lambda k: (gg_line, gg_rx.at[k], x_peers[k]), 0, 3, sems, gg_rx)
    gg_x.start()

    u_sib.arrived()
    for h in range(2):
        q_lo[h].arrived()
    u_all = jnp.concatenate([u[...].reshape(256, FEAT), u_o[...].reshape(256, FEAT)], axis=0)
    q_all = jnp.concatenate(
        [q[...].reshape(256, HID), q_o[...].reshape(256, HID)], axis=0
    )
    first_out[...] = lax.dot_general(u_all, q_all, TN, preferred_element_type=F32).astype(BF16)

    x_own = xp[pl.ds(pl.multiple_of(mine * 8, 8), 8), :]
    f_z.arrived()
    outputs = x_own + z_total(s_fz, r_fz)
    out_ref[0] = outputs[0:4].astype(BF16)
    out_ref[1] = outputs[4:8].astype(BF16)

    g_z.arrived()
    normed_grad = z_total(s_gz, r_gz)
    ee_xh.arrived()
    inner_row = ee_line[:, 128:256] + ee_rx[:, 0:128]
    own_lane = lax.broadcasted_iota(jnp.int32, (8, 128), 1)
    own_spot = lax.broadcasted_iota(jnp.int32, (8, 128), 0) + c * 64 + z * 8
    inner = jnp.sum(
        jnp.where(own_lane == own_spot, jnp.broadcast_to(inner_row, (8, 128)), 0.0),
        axis=1,
        keepdims=True,
    )
    grads = cg[mine].astype(F32) + gain * normed_grad - x_own * inner
    ing_ref[0] = grads[0:4].astype(BF16)
    ing_ref[1] = grads[4:8].astype(BF16)
    gg_x.arrived()
    gg_ref[...] = (gg_line[...] + gg_rx[0]) + (gg_rx[1] + gg_rx[2])

    assert sems["used"] == PHASES
    for phase in sems["phases"][-SENDS:]:
        phase.sent()


def save(*refs):
    sources, targets, sems = refs[:5], refs[5:10], refs[10]
    copies = [pltpu.make_async_copy(sources[i], targets[i], sems.at[i]) for i in range(5)]
    for copy in copies:
        copy.start()
    for copy in copies:
        copy.wait()


def per_device(inputs, gain, w_first, w_second, cotangent):
    vmem = pl.BlockSpec(memory_space=pltpu.VMEM)
    hbm = pl.BlockSpec(memory_space=pltpu.HBM)
    anywhere = pl.BlockSpec(memory_space=pl.ANY)
    shapes = [
        ((2, 128, FEAT), BF16),
        ((1, FEAT), F32),
        ((FEAT, HID), BF16),
        ((HID, FEAT), BF16),
        ((2, 4, FEAT), BF16),
        ((256, FEAT), F32),
        ((2, 128, FEAT), BF16),
        ((2, 128, FEAT), BF16),
        ((32, 8, FEAT), BF16),
        ((32, 8, FEAT), BF16),
        ((2, 128, HID), BF16),
        ((N, 2, 16, HID), BF16),
        ((8, 128), F32),
        ((N, 8, 128), F32),
        ((2, 128, HID), BF16),
        ((2, N, 16, HID), BF16),
        ((2, 128, HID), BF16),
        ((2, 128, HID), BF16),
        ((2, 128, HID), BF16),
        ((2, 128, HID), BF16),
        ((2, 16, HID), F32),
        ((2, 16, HID), F32),
        ((2, 16, 128), F32),
        ((2, 128, FEAT), F32),
        ((2, 64, FEAT), F32),
        ((N, 8, FEAT), BF16),
        ((N, 8, FEAT), BF16),
        ((64, FEAT), BF16),
        ((64, FEAT), BF16),
        ((2, 128, FEAT), F32),
        ((2, 64, FEAT), F32),
        ((N, 8, FEAT), BF16),
        ((N, 8, FEAT), BF16),
        ((64, FEAT), BF16),
        ((64, FEAT), BF16),
        ((1, 256), F32),
        ((N, 1, 256), F32),
        ((1, 256), F32),
        ((1, 256), F32),
        ((1, 256), F32),
        ((N, 1, 256), F32),
        ((1, 256), F32),
        ((1, 256), F32),
        ((1, FEAT), F32),
        ((1, FEAT), F32),
        ((1, FEAT), F32),
        ((N, 1, FEAT), F32),
        ((1, FEAT), F32),
        ((3, 1, FEAT), F32),
    ]
    results = (
        jax.ShapeDtypeStruct(cotangent.shape, BF16),
        jax.ShapeDtypeStruct(cotangent.shape, BF16),
        jax.ShapeDtypeStruct(w_first.shape, BF16),
        jax.ShapeDtypeStruct(w_second.shape, BF16),
        jax.ShapeDtypeStruct((1, FEAT), F32),
    )
    made = pl.pallas_call(
        kernel,
        out_shape=results,
        in_specs=[hbm] * 5,
        out_specs=(vmem,) * 5,
        scratch_shapes=[pltpu.VMEM(shape, dtype) for shape, dtype in shapes]
        + [
            pltpu.SemaphoreType.DMA((SENDS,)),
            pltpu.SemaphoreType.DMA((PHASES,)),
            pltpu.SemaphoreType.DMA((5,)),
        ],
        compiler_params=pltpu.CompilerParams(
            collective_id=0, has_side_effects=True, vmem_limit_bytes=48 * 1024 * 1024
        ),
    )(
        *(
            pltpu.with_memory_space_constraint(array, pltpu.HBM)
            for array in (inputs, gain.reshape(1, FEAT), w_first, w_second, cotangent)
        )
    )
    outputs, input_grad, first_grad, second_grad, gain_grad = pl.pallas_call(
        save,
        out_shape=results,
        in_specs=[vmem] * 5,
        out_specs=(anywhere,) * 5,
        scratch_shapes=[pltpu.SemaphoreType.DMA((5,))],
        compiler_params=pltpu.CompilerParams(vmem_limit_bytes=4 * 1024 * 1024),
    )(*(pltpu.with_memory_space_constraint(array, pltpu.VMEM) for array in made))
    return outputs, input_grad, first_grad, second_grad, gain_grad.reshape(FEAT)


def solution(mesh):
    in_specs = (
        P(None, "section", "tensor"),
        P("tensor"),
        P("tensor", "dp"),
        P("dp", "tensor"),
        P(None, ("section", "dp"), "tensor"),
    )
    out_specs = (
        P(None, ("section", "dp"), "tensor"),
        P(None, ("section", "dp"), "tensor"),
        P("tensor", "dp"),
        P("dp", "tensor"),
        P("tensor"),
    )
    return jax.shard_map(
        per_device, mesh=mesh, in_specs=in_specs, out_specs=out_specs, check_vma=False
    )
```

```python
import jax
import jax.numpy as jnp
from jax import lax
from jax.experimental import pallas as pl
from jax.experimental.pallas import tpu as pltpu
from jax.sharding import PartitionSpec as P

MESH = pl.DeviceIdType.MESH
F32 = jnp.float32
BF16 = jnp.bfloat16
D = 8192
EPSILON = 1e-06
N = 8
HID = 512
FEAT = 1024
NT = (((1,), (1,)), ((), ()))
TN = (((0,), (0,)), ((), ()))


class Phase:
    def __init__(self, make, first, last, sems, whole=None):
        self.make, self.first, self.last, self.sems, self.whole = make, first, last, sems, whole
        self.place = sems["used"]
        sems["used"] += 1

    def describe(self, src, dst, device):
        return pltpu.make_async_remote_copy(
            src_ref=src,
            dst_ref=dst,
            send_sem=self.sems["send"].at[self.send_place],
            recv_sem=self.sems["recv"].at[self.place],
            device_id=device,
            device_id_type=MESH,
        )

    def start(self):
        phases = self.sems["phases"]
        self.send_place = len(phases) % SENDS
        if len(phases) >= SENDS:
            phases[-SENDS].sent()
        phases.append(self)
        order = FARTHEST_FIRST if self.last == N else range(self.first, self.last)
        for k in order:
            self.describe(*self.make(k)).start()

    def all(self):
        src, dst, device = self.make(self.first)
        if self.whole is not None:
            src = dst = self.whole
        return self.describe(src, dst, device)

    def arrived(self):
        self.all().wait_recv()

    def sent(self):
        self.all().wait_send()


SENDS = 16
FAR = (3, N - 3, 1, N - 1)
FARTHEST_FIRST = (3, 5, 4, 2, 6, 1, 7)
PHASES = 40


def kernel(
    x_hbm, gain_hbm, w1_hbm, w2_hbm, cot_hbm,
    out_ref, ing_ref, first_out, second_out, gg_ref,
    x_in, gain_ref, w1, w2, cot_ref, xp, u, u_o, cg, cg_o,
    s_a, r_a, s_sq, r_sq, s_c, r_c, hid, hid_o, q, q_o, p_own, slope, scl,
    branch, r_fs, s_fz, r_fz, r_ff, r_f2, s_fx, r_fx,
    big, r_gs, s_gz, r_gz, s_gx, r_gx,
    e_s, e_r, ee_own, ee_r1, ee_chip, ee_rz, ee_line, ee_rx, gg_own, gg_r1, gg_chip, gg_rz, gg_line, gg_rx,
    send_sems, recv_sems, local_sems,
):
    s = lax.axis_index("section")
    d = lax.axis_index("dp")
    t = lax.axis_index("tensor")
    xh = d // 16
    z = lax.rem(d // 2, N)
    c = lax.rem(d, 2)

    def y_peer(k):
        return {"section": s, "dp": d, "tensor": lax.rem(t + k, N)}

    def z_place(k):
        return lax.rem(z + k, N)

    def z_peer(k):
        return {"section": s, "dp": xh * 16 + z_place(k) * 2 + c, "tensor": t}

    xh_peer = {"section": s, "dp": lax.rem(d + 16, 32), "tensor": t}
    sib_peer = {"section": s, "dp": d + 1 - 2 * c, "tensor": t}
    lo_peer = {"section": 1 - s, "dp": d, "tensor": t}
    far_peer = {"section": 1 - s, "dp": lax.rem(d + 16, 32), "tensor": t}

    sems = {"used": 0, "send": send_sems, "recv": recv_sems, "phases": []}

    load_cot = pltpu.make_async_copy(cot_hbm, cot_ref, local_sems.at[0])
    load_gain = pltpu.make_async_copy(gain_hbm, gain_ref, local_sems.at[1])
    load_x = pltpu.make_async_copy(x_hbm, x_in, local_sems.at[2])
    load_w1 = pltpu.make_async_copy(w1_hbm, w1, local_sems.at[3])
    load_w2 = pltpu.make_async_copy(w2_hbm, w2, local_sems.at[4])
    for load in (load_cot, load_gain, load_x, load_w1, load_w2):
        load.start()

    barrier = pltpu.get_barrier_semaphore()

    def greet(k, carry):
        pl.semaphore_signal(barrier, inc=1, device_id=y_peer(k), device_id_type=MESH)
        pl.semaphore_signal(barrier, inc=1, device_id=z_peer(k), device_id_type=MESH)
        return carry

    lax.fori_loop(1, N, greet, 0)
    for peer in (xh_peer, sib_peer, lo_peer, far_peer):
        pl.semaphore_signal(barrier, inc=1, device_id=peer, device_id_type=MESH)

    def y_rows(k):
        return pl.ds(pl.multiple_of(16 * lax.rem(t + k, N), 16), 16)

    my_rows = y_rows(0)
    mine = 16 + c * 8 + z
    other = c * 8 + z

    load_cot.wait()
    cot_own = jnp.concatenate([cot_ref[0].astype(F32), cot_ref[1].astype(F32)], axis=0)
    cg[mine] = cot_own.astype(BF16)

    row = lax.broadcasted_iota(jnp.int32, (256, 256), 0)
    col = lax.broadcasted_iota(jnp.int32, (256, 256), 1)
    x_half = jnp.where(row // 128 == 1, xh, 1 - xh)
    owner = x_half * 16 + (lax.rem(row, 64) // 8) * 2 + lax.rem(row, 128) // 64
    token = (lax.rem(row, 8) // 4) * 128 + owner * 4 + lax.rem(row, 4)
    perm = jnp.where(col == token, 1.0, 0.0).astype(BF16)
    load_x.wait()
    x_flat = x_in[...].reshape(256, FEAT)
    xs = jnp.dot(perm, x_flat, preferred_element_type=F32)
    xp[...] = xs
    load_gain.wait()
    gain = gain_ref[...]
    u[...] = (xs * gain).astype(BF16).reshape(2, 128, FEAT)
    load_w1.wait()
    s_a[...] = (
        jnp.dot(u[...].reshape(256, FEAT), w1[...], preferred_element_type=F32)
        .astype(BF16)
        .reshape(2, 128, HID)
    )
    pl.semaphore_wait(barrier, 2 * (N - 1) + 4)
    a_y = Phase(lambda k: (s_a.at[:, y_rows(k)], r_a.at[k], y_peer(k)), 1, N, sems, r_a.at[pl.ds(1, N - 1)])
    a_y.start()
    to_xh = Phase(lambda k: (cg.at[mine], cg.at[other], xh_peer), 0, 1, sems)
    to_xh.start()
    to_z = Phase(lambda k: (cg.at[mine], cg.at[mine], z_peer(k)), 1, N, sems, cg.at[pl.ds(0, N - 1)])
    to_z.start()

    ones = jnp.ones((8, FEAT), BF16)
    squares = []
    for h in range(2):
        rows = xp[h * 128 : (h + 1) * 128, :]
        sq = rows * rows
        hi = sq.astype(BF16)
        lo = (sq - hi.astype(F32)).astype(BF16)
        squares.append(
            lax.dot_general(ones, hi, NT, preferred_element_type=F32)
            + lax.dot_general(ones, lo, NT, preferred_element_type=F32)
        )
    place = lax.broadcasted_iota(jnp.int32, (8, 128), 0)
    s_sq[...] = jnp.where(place == 0, squares[0], squares[1])
    sq_y = Phase(lambda k: (s_sq, r_sq.at[k], y_peer(k)), 1, N, sems, r_sq.at[pl.ds(1, N - 1)])
    sq_y.start()

    to_xh.arrived()
    to_z2 = Phase(lambda k: (cg.at[other], cg.at[other], z_peer(k)), 1, N, sems, cg.at[pl.ds(0, N - 1)])
    to_z2.start()
    core_rows = pl.ds(pl.multiple_of(64 * c, 64), 64)
    u_lo = Phase(lambda k: (u.at[:, core_rows], u_o.at[:, core_rows], lo_peer), 0, 1, sems)
    u_lo.start()

    def pieces(h):
        return pl.ds(h * 16 + c * 8, 8)

    def gathered(h):
        return Phase(lambda k: (cg.at[pieces(h)], cg.at[pieces(h)], sib_peer), 0, 1, sems)

    def crossed(h):
        return Phase(lambda k: (cg.at[pieces(h)], cg_o.at[pieces(h)], lo_peer), 0, 1, sems)

    def rows_of(pieces_ref, h):
        return pieces_ref[h * 16 : (h + 1) * 16].astype(F32).reshape(128, FEAT).astype(BF16)

    c_y = [
        Phase(
            lambda k, h=h: (s_c.at[h, y_rows(k)], r_c.at[h, k], y_peer(k)),
            1,
            N,
            sems,
            r_c.at[h, pl.ds(1, N - 1)],
        )
        for h in range(2)
    ]

    def send_c(h):
        s_c[h] = lax.dot_general(
            rows_of(cg, h), w2[...], NT, preferred_element_type=F32
        ).astype(BF16)
        c_y[h].start()

    load_w2.wait()
    to_z.arrived()
    cot_sib1 = gathered(1)
    cot_sib1.start()
    cot_sib1.arrived()
    send_c(1)
    cot_lo1 = crossed(1)
    cot_lo1.start()

    sq_y.arrived()
    total_sq = s_sq[...]
    for k in range(1, N):
        total_sq = total_sq + r_sq[k]
    lane = lax.broadcasted_iota(jnp.int32, (16, 128), 1)
    spot = lax.broadcasted_iota(jnp.int32, (16, 128), 0) + 16 * t
    a_y.arrived()
    for h in range(2):
        picked = jnp.where(lane == spot, jnp.broadcast_to(total_sq[h : h + 1, :], (16, 128)), 0.0)
        scale = lax.rsqrt(jnp.sum(picked, axis=1, keepdims=True) / D + EPSILON)
        sums = s_a[h, my_rows].astype(F32)
        for k in range(1, N):
            sums = sums + r_a[k, h].astype(F32)
        pre = sums * scale
        sig = jax.nn.sigmoid(pre)
        hid[h, my_rows] = (pre * sig).astype(BF16)
        p_own[h] = sums
        slope[h] = sig * (1.0 + pre * (1.0 - sig))
        scl[h] = jnp.broadcast_to(scale, (16, 128))

    b_near = Phase(
        lambda k: (hid.at[:, my_rows], hid.at[:, my_rows], y_peer(1 + 6 * k)),
        0,
        2,
        sems,
        hid.at[:, pl.ds(0, 32)],
    )
    b_near.start()

    to_z2.arrived()
    cot_sib0 = gathered(0)
    cot_sib0.start()
    cot_sib0.arrived()
    send_c(0)
    cot_lo0 = crossed(0)
    cot_lo0.start()

    b_near.arrived()

    def pass_on(k):
        side, step = k // 2, k % 2 + 1
        rows = y_rows(1 if side else N - 1)
        return hid.at[:, rows], hid.at[:, rows], y_peer(N - step if side else step)

    def pass_far(k):
        rows = y_rows(1 if k else N - 1)
        return hid.at[k, rows], hid.at[k, rows], y_peer(N - 3 if k else 3)

    b_rest = (
        Phase(pass_far, 0, 2, sems, hid.at[0, pl.ds(0, 32)]),
        Phase(pass_on, 0, 4, sems, hid.at[:, pl.ds(0, 64)]),
    )
    for phase in b_rest:
        phase.start()

    d_y = [
        Phase(
            lambda k, h=h: (q.at[h, my_rows], q.at[h, my_rows], y_peer(k)),
            1,
            N,
            sems,
            q.at[h, pl.ds(0, 16 * (N - 1))],
        )
        for h in range(2)
    ]
    for h in (1, 0):
        c_y[h].arrived()
        sums = s_c[h, my_rows].astype(F32)
        for k in range(1, N):
            sums = sums + r_c[h, k].astype(F32)
        scale = scl[h][:, :1]
        own = sums * slope[h] * scale
        q[h, my_rows] = own.astype(BF16)
        if h == 0:
            d_y[0].start()
        inner = jnp.sum(own * p_own[h], axis=1, keepdims=True) * (scale * scale / D)
        e_s[:, h * 128 : (h + 1) * 128] = jnp.sum(
            jnp.where(lane == spot, inner, 0.0), axis=0, keepdims=True
        )
    e_y = Phase(lambda k: (e_s, e_r.at[k], y_peer(k)), 1, N, sems, e_r.at[pl.ds(1, N - 1)])
    e_y.start()
    d_y[1].start()

    for phase in b_rest:
        phase.arrived()
    hid_lo = Phase(lambda k: (hid, hid_o, lo_peer), 0, 1, sems)
    hid_lo.start()
    branch[...] = jnp.dot(
        hid[...].reshape(256, HID), w2[...], preferred_element_type=F32
    ).reshape(2, 128, FEAT)
    sib_rows = pl.ds(pl.multiple_of(64 - 64 * c, 64), 64)
    f_sib = Phase(lambda k: (branch.at[:, sib_rows], r_fs, sib_peer), 0, 1, sems)
    f_sib.start()

    u_lo.arrived()
    u_sib = Phase(lambda k: (u_o.at[:, core_rows], u_o.at[:, core_rows], sib_peer), 0, 1, sems)
    u_sib.start()

    f_sib.arrived()
    for h in range(2):
        both = branch[h, core_rows] + r_fs[h]
        s_fz[h] = both.reshape(N, 8, FEAT).astype(BF16)

    def f_near(k):
        step = N - 1 if k % 2 else 1
        if k < 2:
            return s_fz.at[:, z_place(2 * step)], r_fz.at[k], z_peer(step)
        return s_fz.at[k - 2, z_place(4)], r_ff.at[k - 2], z_peer(step)

    f_one = Phase(f_near, 0, 2, sems, r_fz)
    f_one.start()
    f_four = Phase(lambda k: f_near(k + 2), 0, 2, sems, r_ff)
    f_four.start()

    g_sibs = [
        Phase(lambda k, h=h: (big.at[h, sib_rows], r_gs.at[h], sib_peer), 0, 1, sems)
        for h in range(2)
    ]
    g_zs = [
        Phase(
            lambda k, h=h: (s_gz.at[h, z_place(k)], r_gz.at[h, k], z_peer(k)),
            1,
            N,
            sems,
            r_gz.at[h, pl.ds(1, N - 1)],
        )
        for h in range(2)
    ]
    q_lo = [
        Phase(lambda k, h=h: (q.at[h], q_o.at[h], lo_peer), 0, 1, sems)
        for h in range(2)
    ]
    f_far = Phase(
        lambda k: (s_fz.at[:, z_place(FAR[k])], r_f2.at[k], z_peer(FAR[k])), 0, 4, sems, r_f2
    )

    def pass_f():
        f_one.arrived()
        f_four.arrived()
        for k, step in ((0, 1), (1, N - 1)):
            to = z_place(step)
            for h in range(2):
                s_fz[h, to] = (s_fz[h, to].astype(F32) + r_fz[k, h].astype(F32)).astype(BF16)
            to = z_place(3 * step)
            s_fz[k, to] = (s_fz[k, to].astype(F32) + r_ff[k].astype(F32)).astype(BF16)
        f_far.start()

    ee_sib = Phase(lambda k: (ee_own, ee_r1, sib_peer), 0, 1, sems)
    ee_z = Phase(lambda k: (ee_chip, ee_rz.at[k], z_peer(k)), 1, N, sems, ee_rz.at[pl.ds(1, N - 1)])
    gain_part = jnp.zeros((1, FEAT), F32)
    for h in range(2):
        d_y[h].arrived()
        for rows in (sib_rows, core_rows):
            part = lax.dot_general(q[h, rows], w1[...], NT, preferred_element_type=F32)
            big[h, rows] = part
            if rows is sib_rows:
                g_sibs[h].start()
        if h == 0:
            e_y.arrived()
            e_sum = e_s[...]
            for k in range(1, N):
                e_sum = e_sum + e_r[k]
            ee_own[...] = e_sum
            ee_sib.start()
        q_lo[h].start()
        gain_part = gain_part + jnp.sum(
            big[h] * xp[h * 128 : (h + 1) * 128, :], axis=0, keepdims=True
        )
        if h == 1:
            pass_f()
            gg_own[...] = gain_part
            gg_sib = Phase(lambda k: (gg_own, gg_r1, sib_peer), 0, 1, sems)
            gg_sib.start()
        g_sibs[h].arrived()
        both = big[h, core_rows] + r_gs[h]
        s_gz[h] = both.reshape(N, 8, FEAT).astype(BF16)
        if h == 1:
            gg_sib.arrived()
            gg_chip[...] = gg_own[...] + gg_r1[...]
            gg_z = Phase(
                lambda k: (gg_chip, gg_rz.at[k], z_peer(k)), 1, N, sems, gg_rz.at[pl.ds(1, N - 1)]
            )
            gg_z.start()
        g_zs[h].start()
        if h == 0:
            ee_sib.arrived()
            ee_chip[...] = ee_own[...] + ee_r1[...]
            ee_z.start()

    cot_sibo = [
        Phase(lambda k, h=h: (cg_o.at[pieces(h)], cg_o.at[pieces(h)], sib_peer), 0, 1, sems)
        for h in range(2)
    ]
    cot_lo1.arrived()
    cot_sibo[1].start()
    cot_lo0.arrived()
    cot_sibo[0].start()
    hid_lo.arrived()
    for h in range(2):
        cot_sibo[h].arrived()
    hid_all = jnp.concatenate(
        [hid[...].reshape(256, HID), hid_o[...].reshape(256, HID)], axis=0
    )
    cot_all = jnp.concatenate(
        [rows_of(cg, 0), rows_of(cg, 1), rows_of(cg_o, 0), rows_of(cg_o, 1)], axis=0
    )
    second_out[...] = lax.dot_general(
        hid_all, cot_all, TN, preferred_element_type=F32
    ).astype(BF16)

    def z_total(sent, received, h):
        total = sent[h, z].astype(F32)
        for k in range(1, N):
            total = total + received(k)
        return total

    def f_total(h):
        total = s_fz[h, z].astype(F32)
        for k in range(4):
            total = total + r_f2[k, h].astype(F32)
        return total

    ee_z.arrived()
    ee_total = ee_chip[...]
    for k in range(1, N):
        ee_total = ee_total + ee_rz[k]
    ee_line[...] = ee_total
    ee_xh = Phase(lambda k: (ee_line, ee_rx, xh_peer), 0, 1, sems)
    ee_xh.start()

    f_far.arrived()
    s_fx[...] = f_total(0)
    f_xh = Phase(lambda k: (s_fx, r_fx, xh_peer), 0, 1, sems)
    f_xh.start()
    own_branch = f_total(1)

    g_zs[0].arrived()
    s_gx[...] = z_total(s_gz, lambda k: r_gz[0, k].astype(F32), 0)
    g_xh = Phase(lambda k: (s_gx, r_gx, xh_peer), 0, 1, sems)
    g_xh.start()

    gg_z.arrived()
    gg_total = gg_chip[...]
    for k in range(1, N):
        gg_total = gg_total + gg_rz[k]
    gg_line[...] = gg_total
    x_peers = (xh_peer, lo_peer, far_peer)
    gg_x = Phase(lambda k: (gg_line, gg_rx.at[k], x_peers[k]), 0, 3, sems, gg_rx)
    gg_x.start()

    u_sib.arrived()
    for h in range(2):
        q_lo[h].arrived()
    u_all = jnp.concatenate([u[...].reshape(256, FEAT), u_o[...].reshape(256, FEAT)], axis=0)
    q_all = jnp.concatenate(
        [q[...].reshape(256, HID), q_o[...].reshape(256, HID)], axis=0
    )
    first_out[...] = lax.dot_general(u_all, q_all, TN, preferred_element_type=F32).astype(BF16)

    x_own = xp[pl.ds(pl.multiple_of(mine * 8, 8), 8), :]
    f_xh.arrived()
    outputs = x_own + own_branch + r_fx[...]
    out_ref[0] = outputs[0:4].astype(BF16)
    out_ref[1] = outputs[4:8].astype(BF16)

    g_zs[1].arrived()
    normed_grad = z_total(s_gz, lambda k: r_gz[1, k].astype(F32), 1)
    g_xh.arrived()
    normed_grad = normed_grad + r_gx[...]
    ee_xh.arrived()
    inner_row = ee_line[:, 128:256] + ee_rx[:, 0:128]
    own_lane = lax.broadcasted_iota(jnp.int32, (8, 128), 1)
    own_spot = lax.broadcasted_iota(jnp.int32, (8, 128), 0) + c * 64 + z * 8
    inner = jnp.sum(
        jnp.where(own_lane == own_spot, jnp.broadcast_to(inner_row, (8, 128)), 0.0),
        axis=1,
        keepdims=True,
    )
    grads = cg[mine].astype(F32) + gain * normed_grad - x_own * inner
    ing_ref[0] = grads[0:4].astype(BF16)
    ing_ref[1] = grads[4:8].astype(BF16)
    gg_x.arrived()
    gg_ref[...] = (gg_line[...] + gg_rx[0]) + (gg_rx[1] + gg_rx[2])

    for phase in sems["phases"][-SENDS:]:
        phase.sent()


def save(*refs):
    sources, targets, sems = refs[:5], refs[5:10], refs[10]
    copies = [pltpu.make_async_copy(sources[i], targets[i], sems.at[i]) for i in range(5)]
    for copy in copies:
        copy.start()
    for copy in copies:
        copy.wait()


def per_device(inputs, gain, w_first, w_second, cotangent):
    vmem = pl.BlockSpec(memory_space=pltpu.VMEM)
    hbm = pl.BlockSpec(memory_space=pltpu.HBM)
    anywhere = pl.BlockSpec(memory_space=pl.ANY)
    shapes = [
        ((2, 128, FEAT), BF16),
        ((1, FEAT), F32),
        ((FEAT, HID), BF16),
        ((HID, FEAT), BF16),
        ((2, 4, FEAT), BF16),
        ((256, FEAT), F32),
        ((2, 128, FEAT), BF16),
        ((2, 128, FEAT), BF16),
        ((32, 8, FEAT), BF16),
        ((32, 8, FEAT), BF16),
        ((2, 128, HID), BF16),
        ((N, 2, 16, HID), BF16),
        ((8, 128), F32),
        ((N, 8, 128), F32),
        ((2, 128, HID), BF16),
        ((2, N, 16, HID), BF16),
        ((2, 128, HID), BF16),
        ((2, 128, HID), BF16),
        ((2, 128, HID), BF16),
        ((2, 128, HID), BF16),
        ((2, 16, HID), F32),
        ((2, 16, HID), F32),
        ((2, 16, 128), F32),
        ((2, 128, FEAT), F32),
        ((2, 64, FEAT), F32),
        ((2, N, 8, FEAT), BF16),
        ((2, 2, 8, FEAT), BF16),
        ((2, 8, FEAT), BF16),
        ((4, 2, 8, FEAT), BF16),
        ((8, FEAT), F32),
        ((8, FEAT), F32),
        ((2, 128, FEAT), F32),
        ((2, 64, FEAT), F32),
        ((2, N, 8, FEAT), BF16),
        ((2, N, 8, FEAT), BF16),
        ((8, FEAT), F32),
        ((8, FEAT), F32),
        ((1, 256), F32),
        ((N, 1, 256), F32),
        ((1, 256), F32),
        ((1, 256), F32),
        ((1, 256), F32),
        ((N, 1, 256), F32),
        ((1, 256), F32),
        ((1, 256), F32),
        ((1, FEAT), F32),
        ((1, FEAT), F32),
        ((1, FEAT), F32),
        ((N, 1, FEAT), F32),
        ((1, FEAT), F32),
        ((3, 1, FEAT), F32),
    ]
    results = (
        jax.ShapeDtypeStruct(cotangent.shape, BF16),
        jax.ShapeDtypeStruct(cotangent.shape, BF16),
        jax.ShapeDtypeStruct(w_first.shape, BF16),
        jax.ShapeDtypeStruct(w_second.shape, BF16),
        jax.ShapeDtypeStruct((1, FEAT), F32),
    )
    made = pl.pallas_call(
        kernel,
        out_shape=results,
        in_specs=[hbm] * 5,
        out_specs=(vmem,) * 5,
        scratch_shapes=[pltpu.VMEM(shape, dtype) for shape, dtype in shapes]
        + [
            pltpu.SemaphoreType.DMA((SENDS,)),
            pltpu.SemaphoreType.DMA((PHASES,)),
            pltpu.SemaphoreType.DMA((5,)),
        ],
        compiler_params=pltpu.CompilerParams(
            collective_id=0, has_side_effects=True, vmem_limit_bytes=48 * 1024 * 1024
        ),
    )(
        *(
            pltpu.with_memory_space_constraint(array, pltpu.HBM)
            for array in (inputs, gain.reshape(1, FEAT), w_first, w_second, cotangent)
        )
    )
    outputs, input_grad, first_grad, second_grad, gain_grad = pl.pallas_call(
        save,
        out_shape=results,
        in_specs=[vmem] * 5,
        out_specs=(anywhere,) * 5,
        scratch_shapes=[pltpu.SemaphoreType.DMA((5,))],
        compiler_params=pltpu.CompilerParams(vmem_limit_bytes=4 * 1024 * 1024),
    )(*(pltpu.with_memory_space_constraint(array, pltpu.VMEM) for array in made))
    return outputs, input_grad, first_grad, second_grad, gain_grad.reshape(FEAT)


def solution(mesh):
    in_specs = (
        P(None, "section", "tensor"),
        P("tensor"),
        P("tensor", "dp"),
        P("dp", "tensor"),
        P(None, ("section", "dp"), "tensor"),
    )
    out_specs = (
        P(None, ("section", "dp"), "tensor"),
        P(None, ("section", "dp"), "tensor"),
        P("tensor", "dp"),
        P("dp", "tensor"),
        P("tensor"),
    )
    return jax.shard_map(
        per_device, mesh=mesh, in_specs=in_specs, out_specs=out_specs, check_vma=False
    )
```
